32 devices in a mesh: leaf: 16 (over z, y, core), list: 2 (over x).
Axes of the slice: x: 2, y: 2, z: 4, core: 2. Of those that a mesh axis runs over, the one named last changes fastest.
Arguments:
- points: bfloat16 [32, 65536], P(None, 'leaf')
- charges: bfloat16 [32, 65536], P(None, 'leaf'), may hold values from -0.59765625 to 0.59765625
- leaf_ids: int32 [256, 128], P('leaf'), may hold values from 0 to 255, as said below
- inner_ids: int32 [240, 128], P('leaf'), may hold values from 0 to 255, as said below
- upper_ids_first: int32 [8, 128], replicated, may hold values from 0 to 255, as said below
- upper_ids_second: int32 [4, 128], replicated, may hold values from 0 to 255, as said below
- upper_ids_third: int32 [2, 128], replicated, may hold values from 0 to 255, as said below
- leaf_maps: bfloat16 [256, 128, 256], P('leaf'), may hold values from -0.375 to 0.375
- inner_maps: bfloat16 [240, 128, 256], P('leaf'), may hold values from -0.4375 to 0.4375
- upper_maps_first: bfloat16 [1024, 256], P('leaf'), may hold values from -0.4375 to 0.4375
- upper_maps_second: bfloat16 [512, 256], P('leaf'), may hold values from -0.4375 to 0.4375
- upper_maps_third: bfloat16 [256, 256], P('leaf'), may hold values from -0.4375 to 0.4375
- near_lists: int32 [256, 32], P('leaf', 'list'), may hold values from -1 to 255, as said below
- far_inner: int32 [496, 32], P('leaf', 'list'), may hold values from 0 to 255, as said below
- far_upper_first: int32 [8, 32], P(None, 'list'), may hold values from 0 to 7
- far_upper_second: int32 [4, 32], P(None, 'list'), may hold values from 0 to 3
- far_upper_third: int32 [2, 32], P(None, 'list'), may hold values from 0 to 1
Outputs:
- potentials: float32 [32, 65536], P(None, ('leaf', 'list'))
The draws below stay inside these ranges and needn't reach their ends.
Inputs may be any that keep to these rules, and one draw needn't show every extreme that they name: `leaf_ids`: each row holds 128 distinct columns of its leaf. `inner_ids`: each row holds 128 distinct columns of its node's 2 * 128 child skeleton columns. `upper_ids_first`: each row holds 128 distinct columns of its node's 2 * 128 child skeleton columns. `upper_ids_second`: each row holds 128 distinct columns of its node's 2 * 128 child skeleton columns. `upper_ids_third`: each row holds 128 distinct columns of its node's 2 * 128 child skeleton columns. `near_lists`: each row starts with one or more leaf numbers and is -1 after them; some row has 32 leaf numbers. A leaf number s in row i satisfies |s // 16 - i // 16| <= 1. `far_inner`: an entry s of node i at level l satisfies |s // (16 >> l) - i // (16 >> l)| <= 1, both numbered within level l.
All inputs are finite; a program needn't handle non-finite values.
Results may differ from the reference program's by a relative error of at most 0.01.
Values may be sent and summed in bfloat16 or wider, within the bound.
No kernel may reach another device: no remote copies, remote signals or barrier semaphores. Data moves between devices by JAX's collectives and lax.ppermute only.
A program may use at most 128 MiB of HBM per device.

```python
import jax
import jax.numpy as jnp
from jax import lax

DIM = 32
LEAF = 256
SKEL = 128
RHS = 32
NEAR = 32
FAR = 32
LOCAL = 4
LEAF_DEV = 16
SUBTREES = 16
LEAVES = 256
POINTS = 65536


def draw_points(key, part):
    key_centre, key_spread = jax.random.split(key)
    centres = 0.5 * jax.random.normal(key_centre, (DIM, LEAVES, 1))
    spread = 0.55 * jax.random.normal(key_spread, (DIM, LEAVES, LEAF))
    return (centres + spread).reshape(DIM, POINTS).astype(jnp.bfloat16)


def distinct_prefix(key, row_count, choose_from, keep_count):
    scores = jax.random.randint(key, (row_count, choose_from), 0, 1 << 20) * choose_from
    scores = scores + jnp.arange(choose_from, dtype=jnp.int32)[None, :]
    return jnp.argsort(scores, axis=1, stable=True)[:, :keep_count].astype(jnp.int32)


def draw_leaf_ids(key, part):
    return distinct_prefix(jax.random.fold_in(key, 11), LEAVES, LEAF, SKEL)


def draw_inner_ids(key, part):
    return distinct_prefix(jax.random.fold_in(key, 12), SUBTREES * (LEAF_DEV - 1), 2 * SKEL, SKEL)


def draw_upper_ids_first(key, part):
    return distinct_prefix(jax.random.fold_in(key, 13), SUBTREES // 2, 2 * SKEL, SKEL)


def draw_upper_ids_second(key, part):
    return distinct_prefix(jax.random.fold_in(key, 14), SUBTREES // 4, 2 * SKEL, SKEL)


def draw_upper_ids_third(key, part):
    return distinct_prefix(jax.random.fold_in(key, 15), SUBTREES // 8, 2 * SKEL, SKEL)


def draw_near_lists(key, part):
    key_count, key_side, key_within = jax.random.split(jax.random.fold_in(key, 16), 3)
    leaf_index = jnp.arange(LEAVES, dtype=jnp.int32)
    counts = jax.random.randint(key_count, (LEAVES,), 1, NEAR + 1).at[0].set(NEAR)
    neighbour_side = jax.random.randint(key_side, (LEAVES, NEAR), -1, 2)
    subtree = jnp.clip(leaf_index[:, None] // LEAF_DEV + neighbour_side, 0, SUBTREES - 1)
    within = jax.random.randint(key_within, (LEAVES, NEAR), 0, LEAF_DEV)
    entries = subtree * LEAF_DEV + within
    slot_index = jnp.arange(NEAR, dtype=jnp.int32)
    return jnp.where(slot_index[None, :] < counts[:, None], entries, -1).astype(jnp.int32)


def draw_far_inner(key, part):
    blocks = []
    for degree in range(LOCAL + 1):
        per_tree = LEAF_DEV >> degree
        key_side, key_within = jax.random.split(jax.random.fold_in(key, 100 + degree))
        home_tree = jnp.arange(SUBTREES, dtype=jnp.int32)[:, None, None]
        neighbour_side = jax.random.randint(key_side, (SUBTREES, per_tree, FAR), -1, 2)
        target_tree = jnp.clip(home_tree + neighbour_side, 0, SUBTREES - 1)
        within = jax.random.randint(key_within, (SUBTREES, per_tree, FAR), 0, per_tree)
        blocks.append(target_tree * per_tree + within)
    return jnp.concatenate(blocks, axis=1).reshape(SUBTREES * (2 * LEAF_DEV - 1), FAR).astype(jnp.int32)


def plant(values, stream_key, least, largest):
    longest = values.shape.index(max(values.shape))
    spots = []
    for shift in (0, 1):
        where = [jax.random.randint(jax.random.fold_in(stream_key, axis), (), 0, length) for axis, length in enumerate(values.shape)]
        where[longest] = (where[longest] + shift) % values.shape[longest]
        spots.append(tuple(where))
    return values.at[spots[0]].set(least).at[spots[1]].set(largest)


def levels(key, dims, shards, low, top_value):
    level, own = 1.0, jax.random.fold_in(key, 6)
    for position, shards_of in shards:
        draws = jnp.exp(jax.random.uniform(jax.random.fold_in(own, position), (shards_of,), jnp.float32, low / len(shards), top_value / len(shards)))
        level = level * jnp.repeat(draws, dims[position] // shards_of).reshape([-1 if axis == position else 1 for axis in range(len(dims))])
    return level


def noise(stream_key, dims, scale, reach, shards=(), kind=jnp.bfloat16):
    array = scale * jax.random.normal(stream_key, dims, jnp.float32)
    if shards:
        array = array * levels(stream_key, dims, shards, -0.22, 0.18)
    return jnp.clip(array, -reach, reach).astype(kind)


def setup_inputs(seed: int = 0) -> dict:
    streams_of = jax.random.split(jax.random.key(seed), 18)
    return {
        "points": draw_points(jax.random.fold_in(streams_of[17], 71), 0),
        "charges": noise(streams_of[1], (RHS, POINTS), 0.1, 0.59765625, ((1, 16),)),
        "leaf_ids": draw_leaf_ids(jax.random.fold_in(streams_of[17], 71), 0),
        "inner_ids": draw_inner_ids(jax.random.fold_in(streams_of[17], 71), 0),
        "upper_ids_first": draw_upper_ids_first(jax.random.fold_in(streams_of[17], 71), 0),
        "upper_ids_second": draw_upper_ids_second(jax.random.fold_in(streams_of[17], 71), 0),
        "upper_ids_third": draw_upper_ids_third(jax.random.fold_in(streams_of[17], 71), 0),
        "leaf_maps": noise(streams_of[7], (LEAVES, SKEL, LEAF), LEAF ** -0.5, 0.375, ((0, 16),)),
        "inner_maps": noise(streams_of[8], (SUBTREES * (LEAF_DEV - 1), SKEL, 2 * SKEL), (3 * SKEL // 2) ** -0.5, 0.4375, ((0, 16),)),
        "upper_maps_first": noise(streams_of[9], (SUBTREES // 2 * SKEL, 2 * SKEL), (3 * SKEL // 2) ** -0.5, 0.4375, ((0, 16),)),
        "upper_maps_second": noise(streams_of[10], (SUBTREES // 4 * SKEL, 2 * SKEL), (3 * SKEL // 2) ** -0.5, 0.4375, ((0, 16),)),
        "upper_maps_third": noise(streams_of[11], (SUBTREES // 8 * SKEL, 2 * SKEL), (3 * SKEL // 2) ** -0.5, 0.4375, ((0, 16),)),
        "near_lists": draw_near_lists(jax.random.fold_in(streams_of[17], 71), 0),
        "far_inner": draw_far_inner(jax.random.fold_in(streams_of[17], 71), 0),
        "far_upper_first": plant(jax.random.randint(streams_of[14], (SUBTREES // 2, FAR), 0, SUBTREES // 2), jax.random.fold_in(streams_of[14], 1), 0, (SUBTREES // 2) - 1).astype(jnp.int32),
        "far_upper_second": plant(jax.random.randint(streams_of[15], (SUBTREES // 4, FAR), 0, SUBTREES // 4), jax.random.fold_in(streams_of[15], 1), 0, (SUBTREES // 4) - 1).astype(jnp.int32),
        "far_upper_third": plant(jax.random.randint(streams_of[16], (SUBTREES // 8, FAR), 0, SUBTREES // 8), jax.random.fold_in(streams_of[16], 1), 0, (SUBTREES // 8) - 1).astype(jnp.int32),
    }


def kernel_from(goal_coords, source_coords):
    goal_wide = goal_coords.astype(jnp.float32)
    source_wide = source_coords.astype(jnp.float32)
    goal_norm = jnp.sum(goal_wide * goal_wide, axis=-2)
    source_norm = jnp.sum(source_wide * source_wide, axis=-2)
    cross = jnp.einsum("...da,...db->...ab", goal_wide, source_wide, precision=lax.Precision.HIGHEST)
    distance = goal_norm[..., :, None] + source_norm[..., None, :] - 2.0 * cross
    return jnp.exp(distance * (-3.0 / DIM)).astype(jnp.bfloat16)


def near_field(grid_points, grid_charges, near_lists):
    def one_leaf(leaf_index):
        entries = lax.dynamic_index_in_dim(near_lists, leaf_index, 0, keepdims=False)
        is_live = entries >= 0
        safe_entries = jnp.where(is_live, entries, 0).astype(jnp.int32)
        source_coords = jnp.take(grid_points, safe_entries, axis=1).transpose(1, 0, 2)
        source_loads = jnp.take(grid_charges, safe_entries, axis=1)
        goal_coords = lax.dynamic_index_in_dim(grid_points, leaf_index, 1, keepdims=False)
        goal_coords = jnp.broadcast_to(goal_coords[None], source_coords.shape)
        kernel = kernel_from(goal_coords, source_coords) * is_live[:, None, None].astype(jnp.bfloat16)
        return jnp.einsum("rnb,nab->ra", source_loads.astype(jnp.float32), kernel.astype(jnp.float32),
                          precision=lax.Precision.HIGHEST)

    return lax.map(one_leaf, jnp.arange(LEAVES, dtype=jnp.int32))


def far_field(coords, weights, lists):
    def one_node(node_index):
        entries = lax.dynamic_index_in_dim(lists, node_index, 0, keepdims=False)
        source_coords = jnp.take(coords, entries, axis=0)
        source_loads = jnp.take(weights, entries, axis=0)
        goal_coords = lax.dynamic_index_in_dim(coords, node_index, 0, keepdims=False)
        goal_coords = jnp.broadcast_to(goal_coords[None], source_coords.shape)
        kernel = kernel_from(goal_coords, source_coords)
        return jnp.einsum("frs,fts->rt", source_loads.astype(jnp.float32), kernel.astype(jnp.float32),
                          precision=lax.Precision.HIGHEST)

    return lax.map(one_node, jnp.arange(coords.shape[0], dtype=jnp.int32))


def climb_level(coords, weights, chosen, matrices):
    parents = coords.shape[0] // 2
    joined_coords = coords.reshape(parents, 2, DIM, SKEL).transpose(0, 2, 1, 3).reshape(parents, DIM, 2 * SKEL)
    joined_loads = weights.reshape(parents, 2, RHS, SKEL).transpose(0, 2, 1, 3).reshape(parents, RHS, 2 * SKEL)
    new_coords = jnp.take_along_axis(joined_coords, chosen[:, None, :], axis=2)
    new_loads = jnp.einsum("nrk,nsk->nrs", joined_loads.astype(jnp.float32), matrices.astype(jnp.float32),
                           precision=lax.Precision.HIGHEST).astype(jnp.bfloat16)
    return new_coords, new_loads


def reference(points, charges, leaf_ids, inner_ids, upper_ids_first, upper_ids_second, upper_ids_third,
              leaf_maps, inner_maps, upper_maps_first, upper_maps_second, upper_maps_third,
              near_lists, far_inner, far_upper_first, far_upper_second, far_upper_third):
    grid_points = points.reshape(DIM, LEAVES, LEAF)
    grid_charges = charges.reshape(RHS, LEAVES, LEAF)
    coords_list = [jnp.take_along_axis(grid_points, leaf_ids[None], axis=2).transpose(1, 0, 2)]
    weights_list = [jnp.einsum("rnp,nsp->nrs", grid_charges.astype(jnp.float32), leaf_maps.astype(jnp.float32),
                               precision=lax.Precision.HIGHEST).astype(jnp.bfloat16)]
    inner_rows = inner_ids.reshape(SUBTREES, LEAF_DEV - 1, SKEL)
    inner_mats = inner_maps.reshape(SUBTREES, LEAF_DEV - 1, SKEL, 2 * SKEL)
    far_rows = far_inner.reshape(SUBTREES, 2 * LEAF_DEV - 1, FAR)
    lists_all = []
    maps_all = []
    for degree in range(LOCAL + 1):
        per_tree = LEAF_DEV >> degree
        offset_row = 2 * LEAF_DEV - 2 * per_tree
        lists_all.append(far_rows[:, offset_row:offset_row + per_tree].reshape(-1, FAR))
    for degree in range(1, LOCAL + 1):
        per_tree = LEAF_DEV >> degree
        offset_row = LEAF_DEV - 2 * per_tree
        chosen = inner_rows[:, offset_row:offset_row + per_tree].reshape(-1, SKEL)
        matrices = inner_mats[:, offset_row:offset_row + per_tree].reshape(-1, SKEL, 2 * SKEL)
        maps_all.append(matrices)
        new_coords, new_loads = climb_level(coords_list[-1], weights_list[-1], chosen, matrices)
        coords_list.append(new_coords)
        weights_list.append(new_loads)
    uppers = ((upper_ids_first, upper_maps_first, far_upper_first),
              (upper_ids_second, upper_maps_second, far_upper_second),
              (upper_ids_third, upper_maps_third, far_upper_third))
    for chosen, flat_maps, far_list in uppers:
        matrices = flat_maps.reshape(-1, SKEL, 2 * SKEL)
        maps_all.append(matrices)
        lists_all.append(far_list)
        new_coords, new_loads = climb_level(coords_list[-1], weights_list[-1], chosen, matrices)
        coords_list.append(new_coords)
        weights_list.append(new_loads)
    far_terms = [far_field(coords_list[degree], weights_list[degree], lists_all[degree])
                 for degree in range(len(coords_list))]
    totals = far_terms[-1]
    for degree in range(len(far_terms) - 1, 0, -1):
        spread = jnp.einsum("nrs,nsk->nrk", totals, maps_all[degree - 1].astype(jnp.float32),
                            precision=lax.Precision.HIGHEST)
        parents = spread.shape[0]
        children = spread.reshape(parents, RHS, 2, SKEL).transpose(0, 2, 1, 3).reshape(2 * parents, RHS, SKEL)
        totals = far_terms[degree - 1] + children
    far_leaf = jnp.einsum("nrs,nsp->nrp", totals, leaf_maps.astype(jnp.float32), precision=lax.Precision.HIGHEST)
    near_part = near_field(grid_points, grid_charges, near_lists)
    return (near_part + far_leaf).transpose(1, 0, 2).reshape(RHS, POINTS)
```

```python
import functools
import math

import jax
import jax.numpy as jnp
from jax import lax
from jax.experimental import pallas as pl
from jax.experimental.pallas import tpu as pltpu
from jax.sharding import PartitionSpec as P

BF = jnp.bfloat16
F32 = jnp.float32
NORM_ROWS = 16
VMEM_BYTES = 40 * 2**20


def nt(a, b):
    return lax.dot_general(a, b, (((1,), (1,)), ((), ())), preferred_element_type=F32)


def nn(a, b):
    return jnp.dot(a, b, preferred_element_type=F32)


def pick(coords, ids):
    shape = (coords.shape[1], ids.shape[1])
    hot = (lax.broadcasted_iota(jnp.int32, shape, 0) == ids).astype(BF)
    return nn(coords, hot).astype(BF)


def norm_rows(coords, first):
    wide = coords.astype(F32)
    norm = jnp.sum(wide * wide, axis=0, keepdims=True)
    high = norm.astype(BF).astype(F32)
    rest = norm - high
    middle = rest.astype(BF).astype(F32)
    low = rest - middle
    row = lax.broadcasted_iota(jnp.int32, (NORM_ROWS, coords.shape[1]), 0)
    parts = jnp.where(row == first, high, jnp.where(row == first + 1, middle, low))
    inside = (row >= first) & (row < first + 3)
    ones = (row < 6) & jnp.logical_not(inside)
    return jnp.where(inside, parts, jnp.where(ones, 1.0, 0.0)).astype(BF)


def target_side(coords):
    rows = jnp.concatenate(
        [coords.astype(F32) * -2.0, norm_rows(coords, 0).astype(F32)], axis=0
    )
    depth, count = rows.shape
    padded = jnp.concatenate([rows, jnp.zeros((128 - depth, count), F32)], axis=0)
    return padded.T.astype(BF)[:, :depth]


def kernel_block(goal, source, scale):
    return jnp.exp2(nn(goal, source) * scale).astype(BF)


def halves(value):
    high = value.astype(BF)
    low = (value - high.astype(F32)).astype(BF)
    return jnp.concatenate([high, low], axis=0)


def through(value, matrix):
    count = value.shape[0]
    both = nn(halves(value), matrix)
    return both[:count] + both[count:]


def up_body(levels, points, charges, leaf_ids, inner_ids, leaf_maps, inner_maps, up1, up2, up3, stacks, block):
    leaf_count, skel, leaf_size = leaf_maps.shape
    dim = points.shape[0]
    for i in range(leaf_count):
        cols = slice(i * leaf_size, (i + 1) * leaf_size)
        stacks[i, :dim] = pick(points[:, cols], leaf_ids[i : i + 1])
        stacks[i, dim:] = nt(charges[:, cols], leaf_maps[i]).astype(BF)
    below, here, row = 0, leaf_count, 0
    for degree in range(1, levels + 1):
        for i in range(leaf_count >> degree):
            pair = jnp.concatenate([stacks[below + 2 * i], stacks[below + 2 * i + 1]], axis=1)
            stacks[here + i, :dim] = pick(pair[:dim], inner_ids[row : row + 1])
            stacks[here + i, dim:] = nt(pair[dim:], inner_maps[row]).astype(BF)
            row += 1
        below = here
        here += leaf_count >> degree
    root = stacks[here - 1]
    block[:dim] = jnp.concatenate([root[:dim], root[dim:]], axis=1)
    place = dim
    for part in (up1, up2, up3):
        block[place : place + part.shape[0]] = part[...]
        place += part.shape[0]


def entry_of(chunks, row, slot):
    width = chunks[0].shape[1]
    return chunks[slot // width][row, slot % width]


def near_body(n_chunks, share, scale, spot, *refs):
    chunks = refs[:n_chunks]
    sides = refs[n_chunks : n_chunks + 6]
    out, window, loads = refs[n_chunks + 6 :]
    dim, own_points = sides[1].shape
    total, _, leaf_size = window.shape
    leaf_count = total // 3
    position, member = spot[0], spot[1]
    for side in range(3):
        for i in range(leaf_count):
            cols = slice(i * leaf_size, (i + 1) * leaf_size)
            place = sides[side][:, cols]
            window[side * leaf_count + i, :dim] = place
            window[side * leaf_count + i, dim:] = norm_rows(place, 3)
            loads[side * leaf_count + i] = sides[3 + side][:, cols]
    width = chunks[0].shape[1]

    def one_target(t, _):
        leaf = member * share + t
        goal = target_side(window[leaf_count + leaf, :dim])
        counts = []
        for chunk in chunks:
            count = jnp.int32(0)
            for slot in range(width):
                count += (chunk[leaf, slot] >= 0).astype(jnp.int32)
            counts.append(count)
        live = sum(counts)

        def find(slot):
            entry = jnp.int32(-1)
            first = jnp.int32(0)
            for chunk, count in zip(chunks, counts):
                local = slot - first
                ok = (local >= 0) & (local < count)
                value = chunk[leaf, jnp.clip(local, 0, width - 1)]
                entry = jnp.where(ok, value, entry)
                first = first + count
            ok = entry >= 0
            index = jnp.where(ok, entry - (position - 1) * leaf_count, leaf_count)
            return index, ok

        def pair(step, acc):
            for k in range(2):
                index, ok = find(2 * step + k)
                block = kernel_block(goal, window[index], scale)
                load = jnp.where(ok, loads[index], jnp.zeros((), BF))
                acc = acc + nt(load, block)
            return acc

        acc = lax.fori_loop(0, (live + 1) // 2, pair, jnp.zeros((loads.shape[1], leaf_size), F32))
        out[t] = acc
        return 0

    lax.fori_loop(0, share, one_target, 0)


def far_sum(goal, nodes, index_of, slots, group, dim, scale):
    depth = dim + NORM_ROWS
    acc = None
    for first in range(0, slots, group):
        indices = [index_of(first + k) for k in range(group)]
        block = kernel_block(goal, jnp.concatenate([nodes[i, :depth] for i in indices], axis=1), scale)
        load = jnp.concatenate([nodes[i, depth:] for i in indices], axis=1)
        term = nt(load, block)
        acc = term if acc is None else acc + term
    return acc


def far_body(n_chunks, levels, share, rows_at, group, scale, spot, *refs):
    chunks = refs[:n_chunks]
    sides = refs[n_chunks : n_chunks + 3]
    out, nodes = refs[n_chunks + 3 :]
    per_side, stacked, skel = sides[1].shape
    dim = nodes.shape[1] - NORM_ROWS - (nodes.shape[1] - NORM_ROWS) // 2
    depth = dim + NORM_ROWS
    leaf_count = (per_side + 1) // 2
    position, member = spot[0], spot[1]
    slots = n_chunks * chunks[0].shape[1]

    for side in range(3):
        for i in range(per_side):
            at = side * per_side + i
            place = sides[side][i, :dim]
            nodes[at, :dim] = place
            nodes[at, dim:depth] = norm_rows(place, 3)
            nodes[at, depth:] = sides[side][i, dim:]

    made = 0
    for degree in range(levels + 1):
        per_tree = leaf_count >> degree
        first_row = 2 * leaf_count - 2 * per_tree
        count = max(1, share >> degree)
        start = (member * share) >> degree

        def one_target(t, _, first_row=first_row, per_tree=per_tree, start=start, made=made):
            row = first_row + start + t
            goal = target_side(nodes[per_side + row, :dim])

            def index_of(slot):
                entry = entry_of(chunks, rows_at + row, slot)
                side = entry // per_tree - position + 1
                return side * per_side + first_row + entry % per_tree

            out[made + t] = far_sum(goal, nodes, index_of, slots, group, dim, scale)
            return 0

        lax.fori_loop(0, count, one_target, 0)
        made += count


def down_body(n_chunks, levels, share, rows_at, group, scale, spot, *refs):
    chunks = refs[:n_chunks]
    gathered, ids1, ids2, ids3, far, near, inner_maps, leaf_maps, out, nodes, spread = refs[n_chunks:]
    subtrees = gathered.shape[0]
    leaf_count, skel, leaf_size = leaf_maps.shape
    rhs = far.shape[1]
    dim = nodes.shape[1] - NORM_ROWS - rhs
    depth = dim + NORM_ROWS
    position, member = spot[0], spot[1]
    slots = n_chunks * chunks[0].shape[1]
    all_ids = (ids1, ids2, ids3)

    bases, offsets = [], []
    base, offset = 0, dim
    for level in range(3):
        n_nodes = subtrees >> (level + 1)
        group_size = 2 << level
        rows = skel // group_size
        below = bases[-1] if bases else None
        ids = all_ids[level]

        def one_node(j, _, base=base, offset=offset, group_size=group_size, rows=rows, below=below, ids=ids):
            if below is None:
                left, right = gathered[2 * j, :dim], gathered[2 * j + 1, :dim]
                coords = jnp.concatenate([left[:, :skel], right[:, :skel]], axis=1)
                loads = jnp.concatenate([left[:, skel:], right[:, skel:]], axis=1)
            else:
                pair = jnp.concatenate([nodes[below + 2 * j], nodes[below + 2 * j + 1]], axis=1)
                coords, loads = pair[:dim], pair[depth:]
            matrix = jnp.concatenate(
                [gathered[j * group_size + k, offset : offset + rows] for k in range(group_size)], axis=0
            )
            place = pick(coords, ids[pl.ds(j, 1)])
            nodes[base + j, :dim] = place
            nodes[base + j, dim:depth] = norm_rows(place, 3)
            nodes[base + j, depth:] = nt(loads, matrix).astype(BF)
            return 0

        lax.fori_loop(0, n_nodes, one_node, 0, unroll=min(n_nodes, 8))
        bases.append(base)
        offsets.append(offset)
        base += n_nodes
        offset += rows

    total = None
    row_at = rows_at
    rows_of = []
    for level in range(3):
        rows_of.append(row_at)
        row_at += subtrees >> (level + 1)
    for level in range(2, -1, -1):
        ancestor = position >> (level + 1)
        group_size = 2 << level
        rows = skel // group_size
        goal = target_side(nodes[bases[level] + ancestor, :dim])

        def index_of(slot, level=level, ancestor=ancestor):
            return bases[level] + entry_of(chunks, rows_of[level] + ancestor, slot)

        term = far_sum(goal, nodes, index_of, slots, group, dim, scale)
        total = term if total is None else total + term
        branch = (position >> level) & 1
        cols = pl.ds(pl.multiple_of(branch * skel, skel), skel)
        matrix = jnp.concatenate(
            [
                gathered[ancestor * group_size + k, offsets[level] : offsets[level] + rows, cols]
                for k in range(group_size)
            ],
            axis=0,
        )
        total = through(total, matrix)

    firsts = []
    made = 0
    for degree in range(levels + 1):
        firsts.append(made)
        made += max(1, share >> degree)
    totals = [total + far[firsts[levels]]]
    for degree in range(levels, 0, -1):
        first_row = leaf_count - 2 * (leaf_count >> degree)
        start = (member * share) >> degree
        child_start = (member * share) >> (degree - 1)
        children = max(1, share >> (degree - 1))
        after = []
        if children == 1:
            branch = child_start & 1
            cols = pl.ds(pl.multiple_of(branch * skel, skel), skel)
            after.append(through(totals[0], inner_maps[first_row + start, :, cols]) + far[firsts[degree - 1]])
        else:
            for c in range(children // 2):
                both = through(totals[c], inner_maps[first_row + start + c])
                after.append(both[:, :skel] + far[firsts[degree - 1] + 2 * c])
                after.append(both[:, skel:] + far[firsts[degree - 1] + 2 * c + 1])
        totals = after
    for c in range(share):
        out[:, c * leaf_size : (c + 1) * leaf_size] = (
            through(totals[c], leaf_maps[member * share + c]) + near[c]
        )


def on_device(
    points,
    charges,
    leaf_ids,
    inner_ids,
    upper_ids_first,
    upper_ids_second,
    upper_ids_third,
    leaf_maps,
    inner_maps,
    upper_maps_first,
    upper_maps_second,
    upper_maps_third,
    near_lists,
    far_inner,
    far_upper_first,
    far_upper_second,
    far_upper_third,
):
    dim, local_points = points.shape
    rhs = charges.shape[0]
    leaf_count, skel, leaf_size = leaf_maps.shape
    levels = leaf_count.bit_length() - 1
    per_side = 2 * leaf_count - 1
    stacked = dim + rhs
    depth = dim + NORM_ROWS
    subtrees = lax.axis_size("leaf")
    list_size = lax.axis_size("list")
    share = leaf_count // list_size
    scale = -3.0 / dim * math.log2(math.e)
    targets = sum(max(1, share >> degree) for degree in range(levels + 1))
    rightward = [(i, i + 1) for i in range(subtrees - 1)]
    leftward = [(i + 1, i) for i in range(subtrees - 1)]

    spot = jnp.stack([lax.axis_index("leaf"), lax.axis_index("list")]).astype(jnp.int32)
    mine = jnp.concatenate(
        [near_lists, far_inner, far_upper_first, far_upper_second, far_upper_third], axis=0
    )
    chunks = [mine] + [
        lax.ppermute(mine, "list", [(i, (i + shift) % list_size) for i in range(list_size)])
        for shift in range(1, list_size)
    ]
    upper_rows = leaf_count + far_inner.shape[0]

    points_left = lax.ppermute(points, "leaf", rightward)
    points_right = lax.ppermute(points, "leaf", leftward)
    charges_left = lax.ppermute(charges, "leaf", rightward)
    charges_right = lax.ppermute(charges, "leaf", leftward)

    vmem = pl.BlockSpec(memory_space=pltpu.VMEM)
    smem = pl.BlockSpec(memory_space=pltpu.SMEM)
    params = pltpu.CompilerParams(vmem_limit_bytes=VMEM_BYTES)
    lists = [smem] * (1 + len(chunks))
    block_rows = dim + upper_maps_first.shape[0] + upper_maps_second.shape[0] + upper_maps_third.shape[0]

    stacks, block = pl.pallas_call(
        functools.partial(up_body, levels),
        out_shape=(
            jax.ShapeDtypeStruct((per_side, stacked, skel), BF),
            jax.ShapeDtypeStruct((block_rows, 2 * skel), BF),
        ),
        in_specs=[vmem] * 9,
        out_specs=(vmem, vmem),
        compiler_params=params,
        name="upward",
        cost_estimate=pl.CostEstimate(flops=10**9, bytes_accessed=4 * 10**6, transcendentals=0),
    )(points, charges, leaf_ids, inner_ids, leaf_maps, inner_maps, upper_maps_first, upper_maps_second, upper_maps_third)

    stacks_left = lax.ppermute(stacks, "leaf", rightward)
    stacks_right = lax.ppermute(stacks, "leaf", leftward)
    gathered = lax.all_gather(block, "leaf", axis=0)

    near = pl.pallas_call(
        functools.partial(near_body, len(chunks), share, scale),
        out_shape=jax.ShapeDtypeStruct((share, rhs, leaf_size), F32),
        in_specs=lists + [vmem] * 6,
        out_specs=vmem,
        scratch_shapes=[
            pltpu.VMEM((3 * leaf_count, depth, leaf_size), BF),
            pltpu.VMEM((3 * leaf_count, rhs, leaf_size), BF),
        ],
        compiler_params=params,
        name="near",
        cost_estimate=pl.CostEstimate(flops=10**10, bytes_accessed=4 * 10**6, transcendentals=10**7),
    )(spot, *chunks, points_left, points, points_right, charges_left, charges, charges_right)

    far = pl.pallas_call(
        functools.partial(far_body, len(chunks), levels, share, leaf_count, 4, scale),
        out_shape=jax.ShapeDtypeStruct((targets, rhs, skel), F32),
        in_specs=lists + [vmem] * 3,
        out_specs=vmem,
        scratch_shapes=[pltpu.VMEM((3 * per_side, depth + rhs, skel), BF)],
        compiler_params=params,
        name="far",
        cost_estimate=pl.CostEstimate(flops=10**10, bytes_accessed=4 * 10**6, transcendentals=10**7),
    )(spot, *chunks, stacks_left, stacks, stacks_right)

    upper_nodes = sum(subtrees >> (level + 1) for level in range(3))
    return pl.pallas_call(
        functools.partial(down_body, len(chunks), levels, share, upper_rows, 4, scale),
        out_shape=jax.ShapeDtypeStruct((rhs, share * leaf_size), F32),
        in_specs=lists + [vmem] * 8,
        out_specs=vmem,
        scratch_shapes=[
            pltpu.VMEM((upper_nodes, depth + rhs, skel), BF),
            pltpu.VMEM((8, 128), F32),
        ],
        compiler_params=params,
        name="down",
        cost_estimate=pl.CostEstimate(flops=10**9, bytes_accessed=4 * 10**6, transcendentals=10**6),
    )(spot, *chunks, gathered, upper_ids_first, upper_ids_second, upper_ids_third, far, near, inner_maps, leaf_maps)


def solution(mesh):
    placed = (
        P(None, "leaf"),
        P(None, "leaf"),
        P("leaf", None),
        P("leaf", None),
        P(),
        P(),
        P(),
        P("leaf", None, None),
        P("leaf", None, None),
        P("leaf", None),
        P("leaf", None),
        P("leaf", None),
        P("leaf", "list"),
        P("leaf", "list"),
        P(None, "list"),
        P(None, "list"),
        P(None, "list"),
    )
    return jax.shard_map(
        on_device, mesh=mesh, in_specs=placed, out_specs=P(None, ("leaf", "list")), check_vma=False
    )
```

```python
import functools
import math

import jax
import jax.numpy as jnp
from jax import lax
from jax.experimental import pallas as pl
from jax.experimental.pallas import tpu as pltpu
from jax.sharding import PartitionSpec as P

BF = jnp.bfloat16
F32 = jnp.float32
NORM_ROWS = 16
VMEM_BYTES = 40 * 2**20
UP_VMEM_BYTES = 60 * 2**20
LANES = 128
NEAR_UNIT = 1
FAR_UNIT = 2
NEAR_SIZES = (NEAR_UNIT, 16)
FAR_SIZES = (FAR_UNIT, 16)


def nt(a, b):
    return lax.dot_general(a, b, (((1,), (1,)), ((), ())), preferred_element_type=F32)


def nn(a, b):
    return jnp.dot(a, b, preferred_element_type=F32)


def pick(coords, ids):
    shape = (coords.shape[1], ids.shape[1])
    hot = (lax.broadcasted_iota(jnp.int32, shape, 0) == ids).astype(BF)
    return nn(coords, hot).astype(BF)


def norm_rows(coords, first):
    wide = coords.astype(F32)
    norm = jnp.sum(wide * wide, axis=0, keepdims=True)
    high = norm.astype(BF).astype(F32)
    rest = norm - high
    middle = rest.astype(BF).astype(F32)
    low = rest - middle
    row = lax.broadcasted_iota(jnp.int32, (NORM_ROWS, coords.shape[1]), 0)
    parts = jnp.where(row == first, high, jnp.where(row == first + 1, middle, low))
    inside = (row >= first) & (row < first + 3)
    ones = (row < 6) & jnp.logical_not(inside)
    return jnp.where(inside, parts, jnp.where(ones, 1.0, 0.0)).astype(BF)


def target_side(coords):
    rows = jnp.concatenate(
        [coords.astype(F32) * -2.0, norm_rows(coords, 0).astype(F32)], axis=0
    )
    depth, count = rows.shape
    padded = jnp.concatenate([rows, jnp.zeros((128 - depth, count), F32)], axis=0)
    return padded.T.astype(BF)[:, :depth]


def kernel_block(goal, source, scale):
    return jnp.exp2(nn(goal, source) * scale).astype(BF)


def halves(value):
    high = value.astype(BF)
    low = (value - high.astype(F32)).astype(BF)
    return jnp.concatenate([high, low], axis=0)


def through(value, matrix):
    count = value.shape[0]
    both = nn(halves(value), matrix)
    return both[:count] + both[count:]


def up_body(levels, *refs):
    sources, (bundle, blocks), held, sems = refs[:9], refs[9:11], refs[11:20], refs[20]
    copies = [pltpu.make_async_copy(src, dst, sems.at[i]) for i, (src, dst) in enumerate(zip(sources, held))]
    for copy in copies:
        copy.start()
    points, charges, leaf_ids, inner_ids, leaf_maps, inner_maps = held[:6]
    leaf_count, skel, leaf_size = leaf_maps.shape
    dim = points.shape[0]

    def put(node, place, load):
        cols = slice((node % 2) * skel, (node % 2 + 1) * skel)
        bundle[leaf_count + node // 2, :dim, cols] = place
        bundle[leaf_count + node // 2, dim:, cols] = load

    for i in (0, 2):
        copies[i].wait()
    places = []
    for i in range(leaf_count):
        mine = points[:, i * leaf_size : (i + 1) * leaf_size]
        bundle[i, :dim] = mine
        places.append(pick(mine, leaf_ids[i : i + 1]))
    for i in (1, 4):
        copies[i].wait()
    for i in range(leaf_count):
        mine = charges[:, i * leaf_size : (i + 1) * leaf_size]
        bundle[i, dim:] = mine
        put(i, places[i], nt(mine, leaf_maps[i]).astype(BF))
    for i in (3, 5):
        copies[i].wait()
    below, here, row = 0, leaf_count, 0
    for degree in range(1, levels + 1):
        for i in range(leaf_count >> degree):
            pair = bundle[leaf_count + below // 2 + i]
            put(here + i, pick(pair[:dim], inner_ids[row : row + 1]), nt(pair[dim:], inner_maps[row]).astype(BF))
            row += 1
        below = here
        here += leaf_count >> degree
    for node in range(here, 2 * leaf_count):
        empty = jnp.zeros((dim, skel), BF)
        put(node, empty, jnp.zeros((bundle.shape[1] - dim, skel), BF))
    last = here - 1
    root = bundle[leaf_count + last // 2, :, (last % 2) * skel : (last % 2 + 1) * skel]
    parts = [jnp.concatenate([root[:dim], root[dim:]], axis=1)]
    for i in (6, 7, 8):
        copies[i].wait()
        parts.append(held[i][...])
    whole = jnp.concatenate(parts, axis=0)
    for device in range(blocks.shape[0]):
        blocks[device] = whole


def ceil_to(value, unit):
    return -(-value // unit) * unit


class Plan:
    def __init__(self, leaf_count, share, levels, slots, upper_counts):
        self.leaf_count, self.share, self.levels, self.slots = leaf_count, share, levels, slots
        self.per_side = 2 * leaf_count - 1
        self.counts = [max(1, share >> degree) for degree in range(levels + 1)]
        self.first_rows = [2 * leaf_count - 2 * (leaf_count >> degree) for degree in range(levels + 1)]
        self.targets = sum(self.counts)
        self.far_row = share
        self.upper_row = share + self.targets
        self.rows = self.upper_row + len(upper_counts)
        self.upper_counts = upper_counts
        self.upper_bases = [sum(upper_counts[:i]) for i in range(len(upper_counts))]
        trees = [leaf_count >> degree for degree in range(levels + 1)]
        def room(count, unit):
            return ceil_to(min(slots, count), unit)

        most = [
            share * room(leaf_count, NEAR_UNIT),
            share * room(2 * leaf_count, NEAR_UNIT),
            sum(c * room(t, FAR_UNIT) for c, t in zip(self.counts, trees)),
            sum(c * room(2 * t, FAR_UNIT) for c, t in zip(self.counts, trees)),
            sum(room(c, FAR_UNIT) for c in upper_counts),
        ]
        self.starts, at = [], 0
        for count in most:
            self.starts.append(at)
            at += ceil_to(count, LANES)
        self.table_rows = at // LANES
        self.out_rows = ceil_to(self.table_rows + 1, 8)
        width = max(3 * leaf_count, 3 * self.per_side, sum(upper_counts))
        assert width <= LANES and self.rows <= LANES and slots <= LANES


def table_body(plan, n_chunks, spot, *refs):
    chunks, (out, held) = refs[:n_chunks], refs[n_chunks:]
    position, member = spot[0], spot[1]
    leaf_count, share = plan.leaf_count, plan.share
    held[...] = jnp.full(held.shape, -1, jnp.int32)

    def rows_of(start, count):
        return jnp.concatenate([chunk[pl.ds(start, count)] for chunk in chunks], axis=1)

    slots = plan.slots
    entries = rows_of(member * share, share)
    held[:share, :slots] = jnp.where(entries >= 0, entries - (position - 1) * leaf_count, -1)
    row = plan.far_row
    for degree in range(plan.levels + 1):
        count = plan.counts[degree]
        shift = plan.levels - degree
        entries = rows_of(leaf_count + plan.first_rows[degree] + ((member * share) >> degree), count)
        side = (entries >> shift) - position + 1
        within = entries & ((1 << shift) - 1)
        held[row : row + count, :slots] = side * plan.per_side + plan.first_rows[degree] + within
        row += count
    at = leaf_count + plan.per_side
    for level, count in enumerate(plan.upper_counts):
        entries = rows_of(at + (position >> (level + 1)), 1)
        held[row : row + 1, :slots] = entries + plan.upper_bases[level]
        row += 1
        at += count

    across = held[...].astype(F32).T
    square = (LANES, LANES)
    down_i = lax.broadcasted_iota(jnp.int32, square, 0)
    across_i = lax.broadcasted_iota(jnp.int32, square, 1)
    source = down_i.astype(F32)
    often = jnp.zeros(square, F32)
    for k in range(slots):
        often += jnp.where(across[k : k + 1] == source, 1.0, 0.0)
    near_r, far_r = plan.far_row, plan.upper_row
    half = jnp.where(across_i < near_r, leaf_count, plan.per_side)
    inside = (down_i >= half) & (down_i < 2 * half)
    own = (inside & (across_i < far_r)) | ((across_i >= far_r) & (across_i < plan.rows))
    present = often > 0.0
    is_own = jnp.where(present & own, 1.0, 0.0)
    is_rim = jnp.where(present & jnp.logical_not(own), 1.0, 0.0)
    before = jnp.where(across_i < down_i, 1.0, 0.0).astype(BF)
    kind_down = (down_i >= near_r).astype(jnp.int32) + (down_i >= far_r).astype(jnp.int32)
    kind_across = (across_i >= near_r).astype(jnp.int32) + (across_i >= far_r).astype(jnp.int32)
    earlier = jnp.where((down_i < across_i) & (kind_down == kind_across), 1.0, 0.0).astype(BF)
    row_kind = kind_across[:1]
    lane = across_i[:1]
    totals = []
    rank = jnp.zeros(square, F32)
    for mask, starts in ((is_own, (0, 2, 4)), (is_rim, (1, 3, 4))):
        unit = jnp.where(row_kind == 0, float(NEAR_UNIT), float(FAR_UNIT))
        sums = jnp.sum(mask, axis=0, keepdims=True)
        sums = jnp.floor((sums + (unit - 1.0)) / unit) * unit
        base = nn(jnp.broadcast_to(sums, (16, LANES)).astype(BF), earlier)[:1]
        first = jnp.where(
            row_kind == 0,
            float(plan.starts[starts[0]]),
            jnp.where(row_kind == 1, float(plan.starts[starts[1]]), float(plan.starts[starts[2]])),
        )
        rank += mask * (nn(before, mask.astype(BF)) + base + first)
        for kind in range(3):
            totals.append(jnp.sum(jnp.where(row_kind == kind, sums, 0.0), axis=1, keepdims=True))
    spot_of = jnp.where(present & (across_i < plan.rows), rank, -1.0)
    spot_by_row = spot_of.T
    often_by_row = often.T
    part_rows = ceil_to(3 * plan.table_rows, 16)
    shape = (part_rows, LANES)
    part_i = lax.broadcasted_iota(jnp.int32, shape, 0)
    source_i = lax.broadcasted_iota(jnp.int32, shape, 1).astype(F32)
    part = (part_i >= plan.table_rows).astype(jnp.int32) + (part_i >= 2 * plan.table_rows).astype(jnp.int32)
    low = ((part_i - part * plan.table_rows) * LANES).astype(F32)
    slot_i = across_i.astype(F32)
    found = jnp.zeros(shape, F32)
    spot_low = spot_of - jnp.floor(spot_of * (1.0 / LANES)) * LANES
    spot_low = jnp.where(spot_of < 0.0, -1.0, spot_low)
    for r in range(plan.rows):
        where_to = spot_by_row[r : r + 1]
        value = jnp.where(part == 0, source_i, jnp.where(part == 1, often_by_row[r : r + 1], float(r)))
        value = jnp.where((where_to >= low) & (where_to < low + LANES), value, 0.0)
        hot = jnp.where(spot_low[:, r : r + 1] == slot_i, 1.0, 0.0).astype(BF)
        found += nn(value.astype(BF), hot)
    found = found.astype(jnp.int32)
    n = plan.table_rows
    out[:n] = found[:n] + found[n : 2 * n] * LANES + found[2 * n : 3 * n] * (LANES * 64)
    counts = jnp.zeros((1, LANES), F32)
    for at, total in enumerate((totals[0], totals[3], totals[1], totals[4], totals[2])):
        counts = jnp.where(lane == at, total, counts)
    out[n : n + 1] = counts.astype(jnp.int32)


def decode(table, at):
    code = table[at // LANES, at % LANES]
    return code & (LANES - 1), ((code >> 7) & 63).astype(F32), code >> 13


def add_items(plan, table, kind, sizes, goals, nodes, dim, scale, acc, first_row, source_base):
    unit, unroll = sizes
    depth = dim + NORM_ROWS
    start = plan.starts[kind]
    total = table[plan.table_rows, kind]
    group = unit * unroll

    def some(step, _):
        terms = []
        for k in range(unroll):
            items = [decode(table, start + step * group + k * unit + u) for u in range(unit)]
            sources = [jnp.maximum(item[0] - source_base(item[0]), 0) for item in items]
            row = jnp.maximum(items[0][2] - first_row, 0)
            places = jnp.concatenate([nodes[source, :depth] for source in sources], axis=1)
            block = jnp.exp2(nn(goals[row], places) * scale)
            if unit > 1:
                width = block.shape[1] // unit
                block = jnp.concatenate(
                    [block[:, u * width : (u + 1) * width] * items[u][1] for u in range(unit)], axis=1
                )
            loads = jnp.concatenate([nodes[source, depth:] for source in sources], axis=1)
            term = nt(loads, block.astype(BF))
            terms.append((row, term if unit > 1 else term * items[0][1]))
        for row, term in terms:
            acc[row] += term
        return 0

    lax.fori_loop(0, (total + group - 1) // group, some, 0)


def load_leaf(nodes, at, both, dim):
    nodes[at, :dim] = both[:dim]
    nodes[at, dim : dim + NORM_ROWS] = norm_rows(both[:dim], 3)
    nodes[at, dim + NORM_ROWS :] = both[dim:]


def load_side(plan, bundle, leaves, nodes, leaf_at, node_at, dim):
    skel = nodes.shape[2]
    for i in range(plan.leaf_count):
        load_leaf(leaves, leaf_at + i, bundle[i], dim)
    for i in range(plan.per_side):
        cols = slice((i % 2) * skel, (i % 2 + 1) * skel)
        load_leaf(nodes, node_at + i, bundle[plan.leaf_count + i // 2, :, cols], dim)


def own_body(plan, dim, scale, spot, table, bundle, near, far, near_goals, far_goals, leaves, nodes):
    member = spot[1]
    leaf_count, share = plan.leaf_count, plan.share
    load_side(plan, bundle, leaves, nodes, 0, 0, dim)
    for t in range(share):
        near_goals[t] = target_side(leaves[member * share + t, :dim])
    made = 0
    for degree in range(plan.levels + 1):
        start = plan.first_rows[degree] + ((member * share) >> degree)
        for t in range(plan.counts[degree]):
            far_goals[made + t] = target_side(nodes[start + t, :dim])
        made += plan.counts[degree]
    near[...] = jnp.zeros_like(near)
    far[...] = jnp.zeros_like(far)
    add_items(plan, table, 0, NEAR_SIZES, near_goals, leaves, dim, scale, near, 0, lambda s: leaf_count)
    add_items(plan, table, 2, FAR_SIZES, far_goals, nodes, dim, scale, far, plan.far_row, lambda s: plan.per_side)


def rim_body(plan, dim, scale, table, left, right, near_in, far_in, near_goals, far_goals, near, far, leaves, nodes):
    leaf_count, per_side = plan.leaf_count, plan.per_side
    load_side(plan, left, leaves, nodes, 0, 0, dim)
    load_side(plan, right, leaves, nodes, leaf_count, per_side, dim)
    near[...] = near_in[...]
    far[...] = far_in[...]

    def rim(count):
        return lambda s: jnp.where(s >= 2 * count, count, 0)

    add_items(plan, table, 1, NEAR_SIZES, near_goals, leaves, dim, scale, near, 0, rim(leaf_count))
    add_items(plan, table, 3, FAR_SIZES, far_goals, nodes, dim, scale, far, plan.far_row, rim(per_side))


def down_body(plan, dim, scale, spot, table, gathered, ids1, ids2, ids3, far, near, inner_maps, leaf_maps, out, nodes, goals, acc):
    leaf_count, skel, leaf_size = leaf_maps.shape
    share, levels = plan.share, plan.levels
    depth = dim + NORM_ROWS
    position, member = spot[0], spot[1]
    all_ids = (ids1, ids2, ids3)

    offsets = []
    offset = dim
    for level, n_nodes in enumerate(plan.upper_counts):
        group_size = 2 << level
        rows = skel // group_size
        base = plan.upper_bases[level]

        def one_node(j, _, level=level, base=base, offset=offset, group_size=group_size, rows=rows):
            if level == 0:
                left, right = gathered[2 * j, :dim], gathered[2 * j + 1, :dim]
                coords = jnp.concatenate([left[:, :skel], right[:, :skel]], axis=1)
                loads = jnp.concatenate([left[:, skel:], right[:, skel:]], axis=1)
            else:
                below = plan.upper_bases[level - 1]
                pair = jnp.concatenate([nodes[below + 2 * j], nodes[below + 2 * j + 1]], axis=1)
                coords, loads = pair[:dim], pair[depth:]
            matrix = jnp.concatenate(
                [gathered[j * group_size + k, offset : offset + rows] for k in range(group_size)], axis=0
            )
            place = pick(coords, all_ids[level][pl.ds(j, 1)])
            nodes[base + j, :dim] = place
            nodes[base + j, dim:depth] = norm_rows(place, 3)
            nodes[base + j, depth:] = nt(loads, matrix).astype(BF)
            return 0

        lax.fori_loop(0, n_nodes, one_node, 0, unroll=min(n_nodes, 8))
        offsets.append(offset)
        offset += rows

    for level in range(len(plan.upper_counts)):
        goals[level] = target_side(nodes[plan.upper_bases[level] + (position >> (level + 1)), :dim])
    acc[...] = jnp.zeros_like(acc)
    add_items(plan, table, 4, FAR_SIZES, goals, nodes, dim, scale, acc, plan.upper_row, lambda s: 0)

    total = None
    for level in range(len(plan.upper_counts) - 1, -1, -1):
        ancestor = position >> (level + 1)
        group_size = 2 << level
        rows = skel // group_size
        total = acc[level] if total is None else total + acc[level]
        branch = (position >> level) & 1
        cols = pl.ds(pl.multiple_of(branch * skel, skel), skel)
        matrix = jnp.concatenate(
            [
                gathered[ancestor * group_size + k, offsets[level] : offsets[level] + rows, cols]
                for k in range(group_size)
            ],
            axis=0,
        )
        total = through(total, matrix)

    firsts = []
    made = 0
    for degree in range(levels + 1):
        firsts.append(made)
        made += max(1, share >> degree)
    totals = [total + far[firsts[levels]]]
    for degree in range(levels, 0, -1):
        first_row = leaf_count - 2 * (leaf_count >> degree)
        start = (member * share) >> degree
        child_start = (member * share) >> (degree - 1)
        children = max(1, share >> (degree - 1))
        after = []
        if children == 1:
            branch = child_start & 1
            cols = pl.ds(pl.multiple_of(branch * skel, skel), skel)
            after.append(through(totals[0], inner_maps[first_row + start, :, cols]) + far[firsts[degree - 1]])
        else:
            for c in range(children // 2):
                both = through(totals[c], inner_maps[first_row + start + c])
                after.append(both[:, :skel] + far[firsts[degree - 1] + 2 * c])
                after.append(both[:, skel:] + far[firsts[degree - 1] + 2 * c + 1])
        totals = after
    for c in range(share):
        out[:, c * leaf_size : (c + 1) * leaf_size] = (
            through(totals[c], leaf_maps[member * share + c]) + near[c]
        )


def on_device(
    points,
    charges,
    leaf_ids,
    inner_ids,
    upper_ids_first,
    upper_ids_second,
    upper_ids_third,
    leaf_maps,
    inner_maps,
    upper_maps_first,
    upper_maps_second,
    upper_maps_third,
    near_lists,
    far_inner,
    far_upper_first,
    far_upper_second,
    far_upper_third,
):
    dim, local_points = points.shape
    rhs = charges.shape[0]
    leaf_count, skel, leaf_size = leaf_maps.shape
    levels = leaf_count.bit_length() - 1
    stacked = dim + rhs
    depth = dim + NORM_ROWS
    subtrees = lax.axis_size("leaf")
    list_size = lax.axis_size("list")
    share = leaf_count // list_size
    scale = -3.0 / dim * math.log2(math.e)
    rightward = [(i, i + 1) for i in range(subtrees - 1)]
    leftward = [(i + 1, i) for i in range(subtrees - 1)]

    spot = jnp.stack([lax.axis_index("leaf"), lax.axis_index("list")]).astype(jnp.int32)
    mine = jnp.concatenate(
        [near_lists, far_inner, far_upper_first, far_upper_second, far_upper_third], axis=0
    )
    chunks = [mine] + [
        lax.ppermute(mine, "list", [(i, (i + shift) % list_size) for i in range(list_size)])
        for shift in range(1, list_size)
    ]
    uppers = (far_upper_first, far_upper_second, far_upper_third)
    plan = Plan(leaf_count, share, levels, list_size * mine.shape[1], [a.shape[0] for a in uppers])

    vmem = pl.BlockSpec(memory_space=pltpu.VMEM)
    smem = pl.BlockSpec(memory_space=pltpu.SMEM)
    anywhere = pl.BlockSpec(memory_space=pl.ANY)
    params = pltpu.CompilerParams(vmem_limit_bytes=VMEM_BYTES)

    def shaped(shape, dtype=BF):
        return jax.ShapeDtypeStruct(shape, dtype)

    def cost(flops, transcendentals=0):
        return pl.CostEstimate(flops=flops, bytes_accessed=4 * 10**6, transcendentals=transcendentals)

    inputs = (points, charges, leaf_ids, inner_ids, leaf_maps, inner_maps, upper_maps_first, upper_maps_second, upper_maps_third)
    block_rows = dim + sum(a.shape[0] for a in inputs[6:])
    bundle, blocks = pl.pallas_call(
        functools.partial(up_body, levels),
        out_shape=(shaped((2 * leaf_count, stacked, leaf_size)), shaped((subtrees, block_rows, 2 * skel))),
        in_specs=[anywhere] * 9,
        out_specs=(vmem, vmem),
        scratch_shapes=[pltpu.VMEM(a.shape, a.dtype) for a in inputs] + [pltpu.SemaphoreType.DMA((9,))],
        compiler_params=pltpu.CompilerParams(vmem_limit_bytes=UP_VMEM_BYTES),
        name="upward",
        cost_estimate=cost(10**9),
    )(*inputs)

    left = lax.ppermute(bundle, "leaf", rightward)
    right = lax.ppermute(bundle, "leaf", leftward)
    gathered = lax.all_to_all(blocks, "leaf", split_axis=0, concat_axis=0, tiled=True)

    table = pl.pallas_call(
        functools.partial(table_body, plan, len(chunks)),
        out_shape=shaped((plan.out_rows, LANES), jnp.int32),
        in_specs=[smem] + [vmem] * len(chunks),
        out_specs=vmem,
        scratch_shapes=[pltpu.VMEM((LANES, LANES), jnp.int32)],
        compiler_params=params,
        name="table",
        cost_estimate=cost(10**9),
    )(spot, *chunks)

    acc_shapes = (shaped((share, rhs, leaf_size), F32), shaped((plan.targets, rhs, skel), F32))
    goal_shapes = (shaped((share, leaf_size, depth)), shaped((plan.targets, skel, depth)))

    def held(sides):
        return [
            pltpu.VMEM((sides * leaf_count, depth + rhs, leaf_size), BF),
            pltpu.VMEM((sides * plan.per_side, depth + rhs, skel), BF),
        ]

    near, far, near_goals, far_goals = pl.pallas_call(
        functools.partial(own_body, plan, dim, scale),
        out_shape=acc_shapes + goal_shapes,
        in_specs=[smem, smem, vmem],
        out_specs=(vmem,) * 4,
        scratch_shapes=held(1),
        compiler_params=params,
        name="own",
        cost_estimate=cost(10**10, 10**7),
    )(spot, table, bundle)

    near, far = pl.pallas_call(
        functools.partial(rim_body, plan, dim, scale),
        out_shape=acc_shapes,
        in_specs=[smem] + [vmem] * 6,
        out_specs=(vmem,) * 2,
        scratch_shapes=held(2),
        compiler_params=params,
        name="rim",
        cost_estimate=cost(2 * 10**10, 10**7),
    )(table, left, right, near, far, near_goals, far_goals)

    return pl.pallas_call(
        functools.partial(down_body, plan, dim, scale),
        out_shape=shaped((rhs, share * leaf_size), F32),
        in_specs=[smem, smem] + [vmem] * 8,
        out_specs=vmem,
        scratch_shapes=[
            pltpu.VMEM((sum(plan.upper_counts), depth + rhs, skel), BF),
            pltpu.VMEM((len(uppers), skel, depth), BF),
            pltpu.VMEM((len(uppers), rhs, skel), F32),
        ],
        compiler_params=params,
        name="down",
        cost_estimate=cost(10**9, 10**6),
    )(spot, table, gathered, upper_ids_first, upper_ids_second, upper_ids_third, far, near, inner_maps, leaf_maps)


def solution(mesh):
    placed = (
        P(None, "leaf"),
        P(None, "leaf"),
        P("leaf", None),
        P("leaf", None),
        P(),
        P(),
        P(),
        P("leaf", None, None),
        P("leaf", None, None),
        P("leaf", None),
        P("leaf", None),
        P("leaf", None),
        P("leaf", "list"),
        P("leaf", "list"),
        P(None, "list"),
        P(None, "list"),
        P(None, "list"),
    )
    return jax.shard_map(
        on_device, mesh=mesh, in_specs=placed, out_specs=P(None, ("leaf", "list")), check_vma=False
    )
```

```python
import functools
import math

import jax
import jax.numpy as jnp
from jax import lax
from jax.experimental import pallas as pl
from jax.experimental.pallas import tpu as pltpu
from jax.sharding import PartitionSpec as P

BF = jnp.bfloat16
F32 = jnp.float32
NORM_ROWS = 16
VMEM_BYTES = 40 * 2**20
UP_VMEM_BYTES = 60 * 2**20
LANES = 128
NEAR_UNIT = 1
FAR_UNIT = 2
NEAR_SIZES = (NEAR_UNIT, 16)
FAR_SIZES = (FAR_UNIT, 16)


def nt(a, b):
    return lax.dot_general(a, b, (((1,), (1,)), ((), ())), preferred_element_type=F32)


def nn(a, b):
    return jnp.dot(a, b, preferred_element_type=F32)


def pick(coords, ids):
    shape = (coords.shape[1], ids.shape[1])
    hot = (lax.broadcasted_iota(jnp.int32, shape, 0) == ids).astype(BF)
    return nn(coords, hot).astype(BF)


def norm_rows(coords, first):
    wide = coords.astype(F32)
    norm = jnp.sum(wide * wide, axis=0, keepdims=True)
    high = norm.astype(BF).astype(F32)
    rest = norm - high
    middle = rest.astype(BF).astype(F32)
    low = rest - middle
    row = lax.broadcasted_iota(jnp.int32, (NORM_ROWS, coords.shape[1]), 0)
    parts = jnp.where(row == first, high, jnp.where(row == first + 1, middle, low))
    inside = (row >= first) & (row < first + 3)
    ones = (row < 6) & jnp.logical_not(inside)
    return jnp.where(inside, parts, jnp.where(ones, 1.0, 0.0)).astype(BF)


def target_side(coords):
    rows = jnp.concatenate(
        [coords.astype(F32) * -2.0, norm_rows(coords, 0).astype(F32)], axis=0
    )
    depth, count = rows.shape
    padded = jnp.concatenate([rows, jnp.zeros((128 - depth, count), F32)], axis=0)
    return padded.T.astype(BF)[:, :depth]


def kernel_block(goal, source, scale):
    return jnp.exp2(nn(goal, source) * scale).astype(BF)


def halves(value):
    high = value.astype(BF)
    low = (value - high.astype(F32)).astype(BF)
    return jnp.concatenate([high, low], axis=0)


def through(value, matrix):
    count = value.shape[0]
    both = nn(halves(value), matrix)
    return both[:count] + both[count:]


def up_body(levels, *refs):
    sources, (bundle, blocks), held, sems = refs[:9], refs[9:11], refs[11:20], refs[20]
    copies = [pltpu.make_async_copy(src, dst, sems.at[i]) for i, (src, dst) in enumerate(zip(sources, held))]
    for copy in copies:
        copy.start()
    points, charges, leaf_ids, inner_ids, leaf_maps, inner_maps = held[:6]
    leaf_count, skel, leaf_size = leaf_maps.shape
    dim = points.shape[0]

    def put(node, place, load):
        cols = slice((node % 2) * skel, (node % 2 + 1) * skel)
        bundle[leaf_count + node // 2, :dim, cols] = place
        bundle[leaf_count + node // 2, dim:, cols] = load

    for i in (0, 2):
        copies[i].wait()
    places = []
    for i in range(leaf_count):
        mine = points[:, i * leaf_size : (i + 1) * leaf_size]
        bundle[i, :dim] = mine
        places.append(pick(mine, leaf_ids[i : i + 1]))
    for i in (1, 4):
        copies[i].wait()
    for i in range(leaf_count):
        mine = charges[:, i * leaf_size : (i + 1) * leaf_size]
        bundle[i, dim:] = mine
        put(i, places[i], nt(mine, leaf_maps[i]).astype(BF))
    for i in (3, 5):
        copies[i].wait()
    below, here, row = 0, leaf_count, 0
    for degree in range(1, levels + 1):
        for i in range(leaf_count >> degree):
            pair = bundle[leaf_count + below // 2 + i]
            put(here + i, pick(pair[:dim], inner_ids[row : row + 1]), nt(pair[dim:], inner_maps[row]).astype(BF))
            row += 1
        below = here
        here += leaf_count >> degree
    for node in range(here, 2 * leaf_count):
        empty = jnp.zeros((dim, skel), BF)
        put(node, empty, jnp.zeros((bundle.shape[1] - dim, skel), BF))
    last = here - 1
    root = bundle[leaf_count + last // 2, :, (last % 2) * skel : (last % 2 + 1) * skel]
    parts = [jnp.concatenate([root[:dim], root[dim:]], axis=1)]
    for i in (6, 7, 8):
        copies[i].wait()
        parts.append(held[i][...])
    whole = jnp.concatenate(parts, axis=0)
    for i in range(blocks.shape[0]):
        blocks[i] = whole


def ceil_to(value, unit):
    return -(-value // unit) * unit


class Plan:
    def __init__(self, leaf_count, share, levels, slots, upper_counts):
        self.leaf_count, self.share, self.levels, self.slots = leaf_count, share, levels, slots
        self.per_side = 2 * leaf_count
        self.counts = [max(1, share >> degree) for degree in range(levels + 1)]
        self.first_rows = [2 * leaf_count - 2 * (leaf_count >> degree) for degree in range(levels + 1)]
        self.targets = sum(self.counts)
        self.far_row = share
        self.upper_row = share + self.targets
        self.rows = self.upper_row + len(upper_counts)
        self.upper_counts = upper_counts
        self.upper_bases = [sum(upper_counts[:i]) for i in range(len(upper_counts))]
        trees = [leaf_count >> degree for degree in range(levels + 1)]
        def room(count, unit):
            return ceil_to(min(slots, count), unit)

        most = [
            share * room(2 * leaf_count, NEAR_UNIT),
            share * room(leaf_count, NEAR_UNIT),
            sum(c * room(2 * t, FAR_UNIT) for c, t in zip(self.counts, trees)),
            sum(c * room(t, FAR_UNIT) for c, t in zip(self.counts, trees)),
            sum(room(c, FAR_UNIT) for c in upper_counts),
        ]
        self.starts, at = [], 0
        for count in most:
            self.starts.append(at)
            at += ceil_to(count, LANES)
        self.table_rows = at // LANES
        self.out_rows = ceil_to(self.table_rows + 1, 8)
        width = max(3 * leaf_count, 3 * self.per_side, sum(upper_counts))
        assert width <= LANES and self.rows <= LANES and slots <= LANES

    def node_at(self, node):
        return (node & 1) * self.leaf_count + (node >> 1)


def table_body(plan, n_chunks, spot, *refs):
    chunks, (out, held) = refs[:n_chunks], refs[n_chunks:]
    position, member = spot[0], spot[1]
    leaf_count, share = plan.leaf_count, plan.share
    held[...] = jnp.full(held.shape, -1, jnp.int32)

    def rows_of(start, count):
        return jnp.concatenate([chunk[pl.ds(start, count)] for chunk in chunks], axis=1)

    def split(entries, shift):
        tree = entries >> shift
        side = jnp.where(tree == position, 0, jnp.where(tree == (position ^ 1), 1, 2))
        return side, entries & ((1 << shift) - 1)

    slots = plan.slots
    entries = rows_of(member * share, share)
    side, within = split(entries, plan.levels)
    held[:share, :slots] = jnp.where(entries >= 0, side * leaf_count + within, -1)
    row = plan.far_row
    for degree in range(plan.levels + 1):
        count = plan.counts[degree]
        entries = rows_of(leaf_count + plan.first_rows[degree] + ((member * share) >> degree), count)
        side, within = split(entries, plan.levels - degree)
        held[row : row + count, :slots] = side * plan.per_side + plan.node_at(plan.first_rows[degree] + within)
        row += count
    at = leaf_count + plan.per_side - 1
    for level, count in enumerate(plan.upper_counts):
        entries = rows_of(at + (position >> (level + 1)), 1)
        held[row : row + 1, :slots] = entries + plan.upper_bases[level]
        row += 1
        at += count

    across = held[...].astype(F32).T
    square = (LANES, LANES)
    down_i = lax.broadcasted_iota(jnp.int32, square, 0)
    across_i = lax.broadcasted_iota(jnp.int32, square, 1)
    source = down_i.astype(F32)
    often = jnp.zeros(square, F32)
    for k in range(slots):
        often += jnp.where(across[k : k + 1] == source, 1.0, 0.0)
    near_r, far_r = plan.far_row, plan.upper_row
    half = jnp.where(across_i < near_r, leaf_count, plan.per_side)
    inside = down_i < 2 * half
    own = (inside & (across_i < far_r)) | ((across_i >= far_r) & (across_i < plan.rows))
    present = often > 0.0
    is_own = jnp.where(present & own, 1.0, 0.0)
    is_rim = jnp.where(present & jnp.logical_not(own), 1.0, 0.0)
    before = jnp.where(across_i < down_i, 1.0, 0.0).astype(BF)
    kind_down = (down_i >= near_r).astype(jnp.int32) + (down_i >= far_r).astype(jnp.int32)
    kind_across = (across_i >= near_r).astype(jnp.int32) + (across_i >= far_r).astype(jnp.int32)
    earlier = jnp.where((down_i < across_i) & (kind_down == kind_across), 1.0, 0.0).astype(BF)
    row_kind = kind_across[:1]
    lane = across_i[:1]
    totals = []
    rank = jnp.zeros(square, F32)
    for mask, starts in ((is_own, (0, 2, 4)), (is_rim, (1, 3, 4))):
        unit = jnp.where(row_kind == 0, float(NEAR_UNIT), float(FAR_UNIT))
        sums = jnp.sum(mask, axis=0, keepdims=True)
        sums = jnp.floor((sums + (unit - 1.0)) / unit) * unit
        base = nn(jnp.broadcast_to(sums, (16, LANES)).astype(BF), earlier)[:1]
        first = jnp.where(
            row_kind == 0,
            float(plan.starts[starts[0]]),
            jnp.where(row_kind == 1, float(plan.starts[starts[1]]), float(plan.starts[starts[2]])),
        )
        rank += mask * (nn(before, mask.astype(BF)) + base + first)
        for kind in range(3):
            totals.append(jnp.sum(jnp.where(row_kind == kind, sums, 0.0), axis=1, keepdims=True))
    spot_of = jnp.where(present & (across_i < plan.rows), rank, -1.0)
    spot_by_row = spot_of.T
    often_by_row = often.T
    part_rows = ceil_to(3 * plan.table_rows, 16)
    shape = (part_rows, LANES)
    part_i = lax.broadcasted_iota(jnp.int32, shape, 0)
    source_i = lax.broadcasted_iota(jnp.int32, shape, 1).astype(F32)
    part = (part_i >= plan.table_rows).astype(jnp.int32) + (part_i >= 2 * plan.table_rows).astype(jnp.int32)
    low = ((part_i - part * plan.table_rows) * LANES).astype(F32)
    slot_i = across_i.astype(F32)
    found = jnp.zeros(shape, F32)
    spot_low = spot_of - jnp.floor(spot_of * (1.0 / LANES)) * LANES
    spot_low = jnp.where(spot_of < 0.0, -1.0, spot_low)
    for r in range(plan.rows):
        where_to = spot_by_row[r : r + 1]
        value = jnp.where(part == 0, source_i, jnp.where(part == 1, often_by_row[r : r + 1], float(r)))
        value = jnp.where((where_to >= low) & (where_to < low + LANES), value, 0.0)
        hot = jnp.where(spot_low[:, r : r + 1] == slot_i, 1.0, 0.0).astype(BF)
        found += nn(value.astype(BF), hot)
    found = found.astype(jnp.int32)
    n = plan.table_rows
    out[:n] = found[:n] + found[n : 2 * n] * LANES + found[2 * n : 3 * n] * (LANES * 64)
    counts = jnp.zeros((1, LANES), F32)
    for at, total in enumerate((totals[0], totals[3], totals[1], totals[4], totals[2])):
        counts = jnp.where(lane == at, total, counts)
    out[n : n + 1] = counts.astype(jnp.int32)


def decode(table, at):
    code = table[at // LANES, at % LANES]
    return code & (LANES - 1), ((code >> 7) & 63).astype(F32), code >> 13


def add_items(plan, table, kind, sizes, goals, nodes, dim, scale, acc, first_row, first_source):
    unit, unroll = sizes
    depth = dim + NORM_ROWS
    start = plan.starts[kind]
    total = table[plan.table_rows, kind]
    group = unit * unroll

    def some(step, _):
        terms = []
        for k in range(unroll):
            items = [decode(table, start + step * group + k * unit + u) for u in range(unit)]
            sources = [jnp.maximum(item[0] - first_source, 0) for item in items]
            row = jnp.maximum(items[0][2] - first_row, 0)
            places = jnp.concatenate([nodes[source, :depth] for source in sources], axis=1)
            block = jnp.exp2(nn(goals[row], places) * scale)
            if unit > 1:
                width = block.shape[1] // unit
                block = jnp.concatenate(
                    [block[:, u * width : (u + 1) * width] * items[u][1] for u in range(unit)], axis=1
                )
            loads = jnp.concatenate([nodes[source, depth:] for source in sources], axis=1)
            term = nt(loads, block.astype(BF))
            terms.append((row, term if unit > 1 else term * items[0][1]))
        for row, term in terms:
            acc[row] += term
        return 0

    lax.fori_loop(0, (total + group - 1) // group, some, 0)


def leaf_copies(plan, bundle, leaves, at, dim, sems):
    some = slice(0, plan.leaf_count)
    there = pl.ds(at, plan.leaf_count)
    return [
        pltpu.make_async_copy(bundle.at[some, 0:dim], leaves.at[there, 0:dim], sems.at[0]),
        pltpu.make_async_copy(bundle.at[some, dim:], leaves.at[there, dim + NORM_ROWS :], sems.at[1]),
    ]


def node_copies(plan, bundle, nodes, at, dim, sems):
    count = plan.leaf_count
    skel = nodes.shape[2]
    copies = []
    for odd in range(2):
        there = pl.ds(at + odd * count, count)
        cols = slice(odd * skel, (odd + 1) * skel)
        copies += [
            pltpu.make_async_copy(bundle.at[count : 2 * count, 0:dim, cols], nodes.at[there, 0:dim], sems.at[2 * odd]),
            pltpu.make_async_copy(
                bundle.at[count : 2 * count, dim:, cols], nodes.at[there, dim + NORM_ROWS :], sems.at[2 * odd + 1]
            ),
        ]
    return copies


def run_copies(copies):
    for copy in copies:
        copy.start()
    for copy in copies:
        copy.wait()


def fill_norms(nodes, dim):
    for i in range(nodes.shape[0]):
        nodes[i, dim : dim + NORM_ROWS] = norm_rows(nodes[i, :dim], 3)


def near_body(plan, dim, scale, spot, table, bundle, pair, column, near, goals, joined, leaves, sems, column_sem):
    move = pltpu.make_async_copy(column, joined, column_sem)
    move.start()
    member = spot[1]
    count, share = plan.leaf_count, plan.share
    run_copies(
        leaf_copies(plan, bundle, leaves, 0, dim, sems.at[0]) + leaf_copies(plan, pair, leaves, count, dim, sems.at[1])
    )
    fill_norms(leaves, dim)
    for t in range(share):
        goals[t] = target_side(leaves[member * share + t, :dim])
    near[...] = jnp.zeros_like(near)
    add_items(plan, table, 0, NEAR_SIZES, goals, leaves, dim, scale, near, 0, 0)
    move.wait()


def far_body(plan, dim, scale, spot, table, bundle, pair, far, goals, nodes, sems):
    member = spot[1]
    run_copies(
        node_copies(plan, bundle, nodes, 0, dim, sems.at[0])
        + node_copies(plan, pair, nodes, plan.per_side, dim, sems.at[1])
    )
    fill_norms(nodes, dim)
    made = 0
    for degree in range(plan.levels + 1):
        start = plan.first_rows[degree] + ((member * plan.share) >> degree)
        for t in range(plan.counts[degree]):
            goals[made + t] = target_side(nodes[plan.node_at(start + t), :dim])
        made += plan.counts[degree]
    far[...] = jnp.zeros_like(far)
    add_items(plan, table, 2, FAR_SIZES, goals, nodes, dim, scale, far, plan.far_row, 0)


def cross_far_body(plan, dim, scale, table, cross, far_in, goals, part, far, passed, nodes, sems, part_sem):
    move = pltpu.make_async_copy(part, passed, part_sem)
    move.start()
    run_copies(node_copies(plan, cross, nodes, 0, dim, sems))
    fill_norms(nodes, dim)
    far[...] = far_in[...]
    add_items(plan, table, 3, FAR_SIZES, goals, nodes, dim, scale, far, plan.far_row, 2 * plan.per_side)
    move.wait()


def cross_near_body(plan, dim, scale, table, cross, near_in, goals, part, near, leaves, sems):
    run_copies(leaf_copies(plan, cross, leaves, 0, dim, sems))
    fill_norms(leaves, dim)
    near[...] = near_in[...]
    add_items(plan, table, 1, NEAR_SIZES, goals, leaves, dim, scale, near, 0, 2 * plan.leaf_count)


def down_body(plan, dim, scale, spot, table, *refs):
    quarters, refs = refs[:4], refs[4:]
    ids1, ids2, ids3, far, near, inner_maps, leaf_maps, out, nodes, goals, acc, gathered, where_is, sems = refs
    quarter = quarters[0].shape[0]
    copies = [
        pltpu.make_async_copy(part, gathered.at[i * quarter : (i + 1) * quarter], sems.at[i])
        for i, part in enumerate(quarters)
    ]
    for copy in copies:
        copy.start()
    leaf_count, skel, leaf_size = leaf_maps.shape
    share, levels = plan.share, plan.levels
    depth = dim + NORM_ROWS
    position, member = spot[0], spot[1]
    all_ids = (ids1, ids2, ids3)

    def find(d, _):
        other = d ^ position
        where_is[d] = (other & 3) * quarter + (d >> 2)
        return 0

    lax.fori_loop(0, gathered.shape[0], find, 0, unroll=16)
    for copy in copies:
        copy.wait()

    offsets = []
    offset = dim
    for level, n_nodes in enumerate(plan.upper_counts):
        group_size = 2 << level
        rows = skel // group_size
        base = plan.upper_bases[level]

        def one_node(j, _, level=level, base=base, offset=offset, group_size=group_size, rows=rows):
            if level == 0:
                left, right = gathered[where_is[2 * j], :dim], gathered[where_is[2 * j + 1], :dim]
                coords = jnp.concatenate([left[:, :skel], right[:, :skel]], axis=1)
                loads = jnp.concatenate([left[:, skel:], right[:, skel:]], axis=1)
            else:
                below = plan.upper_bases[level - 1]
                pair = jnp.concatenate([nodes[below + 2 * j], nodes[below + 2 * j + 1]], axis=1)
                coords, loads = pair[:dim], pair[depth:]
            matrix = jnp.concatenate(
                [gathered[where_is[j * group_size + k], offset : offset + rows] for k in range(group_size)], axis=0
            )
            place = pick(coords, all_ids[level][pl.ds(j, 1)])
            nodes[base + j, :dim] = place
            nodes[base + j, dim:depth] = norm_rows(place, 3)
            nodes[base + j, depth:] = nt(loads, matrix).astype(BF)
            return 0

        lax.fori_loop(0, n_nodes, one_node, 0, unroll=min(n_nodes, 8))
        offsets.append(offset)
        offset += rows

    for level in range(len(plan.upper_counts)):
        goals[level] = target_side(nodes[plan.upper_bases[level] + (position >> (level + 1)), :dim])
    acc[...] = jnp.zeros_like(acc)
    add_items(plan, table, 4, FAR_SIZES, goals, nodes, dim, scale, acc, plan.upper_row, 0)

    total = None
    for level in range(len(plan.upper_counts) - 1, -1, -1):
        ancestor = position >> (level + 1)
        group_size = 2 << level
        rows = skel // group_size
        total = acc[level] if total is None else total + acc[level]
        branch = (position >> level) & 1
        cols = pl.ds(pl.multiple_of(branch * skel, skel), skel)
        matrix = jnp.concatenate(
            [
                gathered[where_is[ancestor * group_size + k], offsets[level] : offsets[level] + rows, cols]
                for k in range(group_size)
            ],
            axis=0,
        )
        total = through(total, matrix)

    firsts = []
    made = 0
    for degree in range(levels + 1):
        firsts.append(made)
        made += max(1, share >> degree)
    totals = [total + far[firsts[levels]]]
    for degree in range(levels, 0, -1):
        first_row = leaf_count - 2 * (leaf_count >> degree)
        start = (member * share) >> degree
        child_start = (member * share) >> (degree - 1)
        children = max(1, share >> (degree - 1))
        after = []
        if children == 1:
            branch = child_start & 1
            cols = pl.ds(pl.multiple_of(branch * skel, skel), skel)
            after.append(through(totals[0], inner_maps[first_row + start, :, cols]) + far[firsts[degree - 1]])
        else:
            for c in range(children // 2):
                both = through(totals[c], inner_maps[first_row + start + c])
                after.append(both[:, :skel] + far[firsts[degree - 1] + 2 * c])
                after.append(both[:, skel:] + far[firsts[degree - 1] + 2 * c + 1])
        totals = after
    for c in range(share):
        out[:, c * leaf_size : (c + 1) * leaf_size] = (
            through(totals[c], leaf_maps[member * share + c]) + near[c]
        )


def on_device(
    points,
    charges,
    leaf_ids,
    inner_ids,
    upper_ids_first,
    upper_ids_second,
    upper_ids_third,
    leaf_maps,
    inner_maps,
    upper_maps_first,
    upper_maps_second,
    upper_maps_third,
    near_lists,
    far_inner,
    far_upper_first,
    far_upper_second,
    far_upper_third,
):
    dim, local_points = points.shape
    rhs = charges.shape[0]
    leaf_count, skel, leaf_size = leaf_maps.shape
    levels = leaf_count.bit_length() - 1
    stacked = dim + rhs
    depth = dim + NORM_ROWS
    subtrees = lax.axis_size("leaf")
    list_size = lax.axis_size("list")
    share = leaf_count // list_size
    scale = -3.0 / dim * math.log2(math.e)
    on_chip = [(i, i ^ 1) for i in range(subtrees)]
    across = [pair for i in range(1, subtrees - 1, 2) for pair in ((i, i + 1), (i + 1, i))]

    spot = jnp.stack([lax.axis_index("leaf"), lax.axis_index("list")]).astype(jnp.int32)
    mine = jnp.concatenate(
        [near_lists, far_inner, far_upper_first, far_upper_second, far_upper_third], axis=0
    )
    chunks = [mine] + [
        lax.ppermute(mine, "list", [(i, (i + shift) % list_size) for i in range(list_size)])
        for shift in range(1, list_size)
    ]
    uppers = (far_upper_first, far_upper_second, far_upper_third)
    plan = Plan(leaf_count, share, levels, list_size * mine.shape[1], [a.shape[0] for a in uppers])

    vmem = pl.BlockSpec(memory_space=pltpu.VMEM)
    smem = pl.BlockSpec(memory_space=pltpu.SMEM)
    anywhere = pl.BlockSpec(memory_space=pl.ANY)
    params = pltpu.CompilerParams(vmem_limit_bytes=VMEM_BYTES)

    def shaped(shape, dtype=BF):
        return jax.ShapeDtypeStruct(shape, dtype)

    def cost(flops, transcendentals=0):
        return pl.CostEstimate(flops=flops, bytes_accessed=4 * 10**6, transcendentals=transcendentals)

    inputs = (points, charges, leaf_ids, inner_ids, leaf_maps, inner_maps, upper_maps_first, upper_maps_second, upper_maps_third)
    block_rows = dim + sum(a.shape[0] for a in inputs[6:])
    bundle, blocks = pl.pallas_call(
        functools.partial(up_body, levels),
        out_shape=(shaped((2 * leaf_count, stacked, leaf_size)), shaped((subtrees // 4, block_rows, 2 * skel))),
        in_specs=[anywhere] * 9,
        out_specs=(vmem, vmem),
        scratch_shapes=[pltpu.VMEM(a.shape, a.dtype) for a in inputs] + [pltpu.SemaphoreType.DMA((9,))],
        compiler_params=pltpu.CompilerParams(vmem_limit_bytes=UP_VMEM_BYTES),
        name="upward",
        cost_estimate=cost(10**9),
    )(*inputs)

    cross = lax.ppermute(bundle, "leaf", across)
    pair = lax.ppermute(bundle, "leaf", on_chip)
    columns = [list(range(i, subtrees, 4)) for i in range(4)]
    column = lax.all_to_all(blocks, "leaf", split_axis=0, concat_axis=0, tiled=True, axis_index_groups=columns)

    table = pl.pallas_call(
        functools.partial(table_body, plan, len(chunks)),
        out_shape=shaped((plan.out_rows, LANES), jnp.int32),
        in_specs=[smem] + [vmem] * len(chunks),
        out_specs=vmem,
        scratch_shapes=[pltpu.VMEM((LANES, LANES), jnp.int32)],
        compiler_params=params,
        name="table",
        cost_estimate=cost(10**9),
    )(spot, *chunks)

    acc_shapes = (shaped((share, rhs, leaf_size), F32), shaped((plan.targets, rhs, skel), F32))
    goal_shapes = (shaped((share, leaf_size, depth)), shaped((plan.targets, skel, depth)))

    def leaves_of(sides):
        return pltpu.VMEM((sides * leaf_count, depth + rhs, leaf_size), BF)

    def nodes_of(sides):
        return pltpu.VMEM((sides * plan.per_side, depth + rhs, skel), BF)

    near, near_goals, joined = pl.pallas_call(
        functools.partial(near_body, plan, dim, scale),
        out_shape=(acc_shapes[0], goal_shapes[0], shaped(column.shape)),
        in_specs=[smem, smem] + [anywhere] * 3,
        out_specs=(vmem, vmem, anywhere),
        scratch_shapes=[leaves_of(2), pltpu.SemaphoreType.DMA((2, 2)), pltpu.SemaphoreType.DMA],
        compiler_params=params,
        name="near",
        cost_estimate=cost(10**10, 10**7),
    )(spot, table, bundle, pair, column)

    def swapped(value, mask):
        return lax.ppermute(value, "leaf", [(i, i ^ mask) for i in range(subtrees)])

    second, third = swapped(joined, 1), swapped(joined, 2)

    far, far_goals = pl.pallas_call(
        functools.partial(far_body, plan, dim, scale),
        out_shape=(acc_shapes[1], goal_shapes[1]),
        in_specs=[smem, smem, anywhere, anywhere],
        out_specs=(vmem,) * 2,
        scratch_shapes=[nodes_of(2), pltpu.SemaphoreType.DMA((2, 4))],
        compiler_params=params,
        name="far",
        cost_estimate=cost(10**10, 10**7),
    )(spot, table, bundle, pair)

    far, passed = pl.pallas_call(
        functools.partial(cross_far_body, plan, dim, scale),
        out_shape=(acc_shapes[1], shaped(third.shape)),
        in_specs=[smem, anywhere, vmem, vmem, anywhere],
        out_specs=(vmem, anywhere),
        scratch_shapes=[nodes_of(1), pltpu.SemaphoreType.DMA((4,)), pltpu.SemaphoreType.DMA],
        compiler_params=params,
        name="crossfar",
        cost_estimate=cost(10**10, 10**7),
    )(table, cross, far, far_goals, third)

    quarters = [joined, second, third, swapped(passed, 1)]

    near = pl.pallas_call(
        functools.partial(cross_near_body, plan, dim, scale),
        out_shape=acc_shapes[0],
        in_specs=[smem, anywhere, vmem, vmem, anywhere],
        out_specs=vmem,
        scratch_shapes=[leaves_of(1), pltpu.SemaphoreType.DMA((2,))],
        compiler_params=params,
        name="crossnear",
        cost_estimate=cost(10**10, 10**7),
    )(table, cross, near, near_goals, passed)

    return pl.pallas_call(
        functools.partial(down_body, plan, dim, scale),
        out_shape=shaped((rhs, share * leaf_size), F32),
        in_specs=[smem, smem] + [anywhere] * 4 + [vmem] * 7,
        out_specs=vmem,
        scratch_shapes=[
            pltpu.VMEM((sum(plan.upper_counts), depth + rhs, skel), BF),
            pltpu.VMEM((len(uppers), skel, depth), BF),
            pltpu.VMEM((len(uppers), rhs, skel), F32),
            pltpu.VMEM((subtrees, block_rows, 2 * skel), BF),
            pltpu.SMEM((subtrees,), jnp.int32),
            pltpu.SemaphoreType.DMA((4,)),
        ],
        compiler_params=params,
        name="down",
        cost_estimate=cost(10**9, 10**6),
    )(spot, table, *quarters, upper_ids_first, upper_ids_second, upper_ids_third, far, near, inner_maps, leaf_maps)


def solution(mesh):
    placed = (
        P(None, "leaf"),
        P(None, "leaf"),
        P("leaf", None),
        P("leaf", None),
        P(),
        P(),
        P(),
        P("leaf", None, None),
        P("leaf", None, None),
        P("leaf", None),
        P("leaf", None),
        P("leaf", None),
        P("leaf", "list"),
        P("leaf", "list"),
        P(None, "list"),
        P(None, "list"),
        P(None, "list"),
    )
    return jax.shard_map(
        on_device, mesh=mesh, in_specs=placed, out_specs=P(None, ("leaf", "list")), check_vma=False
    )
```

```python
import functools
import math

import jax
import jax.numpy as jnp
from jax import lax
from jax.experimental import pallas as pl
from jax.experimental.pallas import tpu as pltpu
from jax.sharding import PartitionSpec as P

BF = jnp.bfloat16
F32 = jnp.float32
NORM_ROWS = 16
VMEM_BYTES = 40 * 2**20
UP_VMEM_BYTES = 60 * 2**20
LANES = 128
NEAR_UNIT = 1
FAR_UNIT = 2
NEAR_SIZES = (NEAR_UNIT, 16)
FAR_SIZES = (FAR_UNIT, 16)


def nt(a, b):
    return lax.dot_general(a, b, (((1,), (1,)), ((), ())), preferred_element_type=F32)


def nn(a, b):
    return jnp.dot(a, b, preferred_element_type=F32)


def pick(coords, ids):
    shape = (coords.shape[1], ids.shape[1])
    hot = (lax.broadcasted_iota(jnp.int32, shape, 0) == ids).astype(BF)
    return nn(coords, hot).astype(BF)


def norm_rows(coords, first):
    wide = coords.astype(F32)
    norm = jnp.sum(wide * wide, axis=0, keepdims=True)
    high = norm.astype(BF).astype(F32)
    rest = norm - high
    middle = rest.astype(BF).astype(F32)
    low = rest - middle
    row = lax.broadcasted_iota(jnp.int32, (NORM_ROWS, coords.shape[1]), 0)
    parts = jnp.where(row == first, high, jnp.where(row == first + 1, middle, low))
    inside = (row >= first) & (row < first + 3)
    ones = (row < 6) & jnp.logical_not(inside)
    return jnp.where(inside, parts, jnp.where(ones, 1.0, 0.0)).astype(BF)


def target_side(coords):
    rows = jnp.concatenate(
        [coords.astype(F32) * -2.0, norm_rows(coords, 0).astype(F32)], axis=0
    )
    depth, count = rows.shape
    padded = jnp.concatenate([rows, jnp.zeros((128 - depth, count), F32)], axis=0)
    return padded.T.astype(BF)[:, :depth]


def kernel_block(goal, source, scale):
    return jnp.exp2(nn(goal, source) * scale).astype(BF)


def halves(value):
    high = value.astype(BF)
    low = (value - high.astype(F32)).astype(BF)
    return jnp.concatenate([high, low], axis=0)


def through(value, matrix):
    count = value.shape[0]
    both = nn(halves(value), matrix)
    return both[:count] + both[count:]


def up_body(levels, *refs):
    sources, (bundle, extras, block), held, sems = refs[:9], refs[9:12], refs[12:21], refs[21]
    copies = [pltpu.make_async_copy(src, dst, sems.at[i]) for i, (src, dst) in enumerate(zip(sources, held))]
    for copy in copies:
        copy.start()
    points, charges, leaf_ids, inner_ids, leaf_maps, inner_maps = held[:6]
    leaf_count, skel, leaf_size = leaf_maps.shape
    dim = points.shape[0]
    quarter = leaf_count // 2

    def put(node, place, load):
        cols = slice((node % 2) * skel, (node % 2 + 1) * skel)
        bundle[leaf_count + node // 2, :dim, cols] = place
        bundle[leaf_count + node // 2, dim:, cols] = load
        rhs = load.shape[0]
        pair, half = node // 2 % quarter, node // 2 // quarter
        extras[pair, half * rhs : (half + 1) * rhs, cols] = load

    for i in (0, 2):
        copies[i].wait()
    places = []
    for i in range(leaf_count):
        mine = points[:, i * leaf_size : (i + 1) * leaf_size]
        bundle[i, :dim] = mine
        places.append(pick(mine, leaf_ids[i : i + 1]))
    for i in (1, 4):
        copies[i].wait()
    for i in range(leaf_count):
        mine = charges[:, i * leaf_size : (i + 1) * leaf_size]
        bundle[i, dim:] = mine
        put(i, places[i], nt(mine, leaf_maps[i]).astype(BF))
    for i in (3, 5):
        copies[i].wait()
    extras[quarter] = jnp.zeros(extras.shape[1:], BF)
    extras[quarter, :leaf_count, :skel] = leaf_ids[...].astype(F32).astype(BF)
    extras[quarter, :leaf_count, skel:] = jnp.concatenate(
        [inner_ids[...], jnp.zeros((1, skel), jnp.int32)], axis=0
    ).astype(F32).astype(BF)
    below, here, row = 0, leaf_count, 0
    for degree in range(1, levels + 1):
        for i in range(leaf_count >> degree):
            pair = bundle[leaf_count + below // 2 + i]
            put(here + i, pick(pair[:dim], inner_ids[row : row + 1]), nt(pair[dim:], inner_maps[row]).astype(BF))
            row += 1
        below = here
        here += leaf_count >> degree
    for node in range(here, 2 * leaf_count):
        empty = jnp.zeros((dim, skel), BF)
        put(node, empty, jnp.zeros((bundle.shape[1] - dim, skel), BF))
    last = here - 1
    root = bundle[leaf_count + last // 2, :, (last % 2) * skel : (last % 2 + 1) * skel]
    parts = [jnp.concatenate([root[:dim], root[dim:]], axis=1)]
    for i in (6, 7, 8):
        copies[i].wait()
        parts.append(held[i][...])
    whole = jnp.concatenate(parts, axis=0)
    block[...] = whole


def ceil_to(value, unit):
    return -(-value // unit) * unit


class Plan:
    def __init__(self, leaf_count, share, levels, slots, upper_counts):
        self.leaf_count, self.share, self.levels, self.slots = leaf_count, share, levels, slots
        self.per_side = 2 * leaf_count
        self.counts = [max(1, share >> degree) for degree in range(levels + 1)]
        self.first_rows = [2 * leaf_count - 2 * (leaf_count >> degree) for degree in range(levels + 1)]
        self.targets = sum(self.counts)
        self.far_row = share
        self.upper_row = share + self.targets
        self.rows = self.upper_row + len(upper_counts)
        self.upper_counts = upper_counts
        self.upper_bases = [sum(upper_counts[:i]) for i in range(len(upper_counts))]
        trees = [leaf_count >> degree for degree in range(levels + 1)]
        def room(count, unit):
            return ceil_to(min(slots, count), unit)

        most = [
            share * room(2 * leaf_count, NEAR_UNIT),
            share * room(leaf_count, NEAR_UNIT),
            sum(c * room(2 * t, FAR_UNIT) for c, t in zip(self.counts, trees)),
            sum(c * room(t, FAR_UNIT) for c, t in zip(self.counts, trees)),
            sum(room(c, FAR_UNIT) for c in upper_counts),
        ]
        self.starts, at = [], 0
        for count in most:
            self.starts.append(at)
            at += ceil_to(count, LANES)
        self.table_rows = at // LANES
        self.out_rows = ceil_to(self.table_rows + 1, 8)
        width = max(3 * leaf_count, 3 * self.per_side, sum(upper_counts))
        assert width <= LANES and self.rows <= LANES and slots <= LANES

    def node_at(self, node):
        return (node & 1) * self.leaf_count + (node >> 1)


def in_order(bit, mine, theirs):
    low = jnp.where(bit == 0, mine, theirs)
    high = jnp.where(bit == 0, theirs, mine)
    return low, high


def climb(low, high, matrix, ids):
    skel = low.shape[1] // 2
    coords = jnp.concatenate([low[:, :skel], high[:, :skel]], axis=1)
    loads = jnp.concatenate([low[:, skel:], high[:, skel:]], axis=1)
    return jnp.concatenate([pick(coords, ids), nt(loads, matrix).astype(BF)], axis=1)


def climb_stage(level, position, dim, sizes, mine, theirs, ids, message, matrix_out):
    bit = (position >> level) & 1
    low, high = in_order(bit, mine[...], theirs[...])
    below = sum(dim << (level - k) for k in range(1, level + 1)) if level else dim
    nodes_low, nodes_high = low[:below], high[:below]
    at = below
    maps = []
    for rows in sizes[level:]:
        rows = rows << level
        maps.append(jnp.concatenate([low[at : at + rows], high[at : at + rows]], axis=0))
        at += rows
    matrix_out[...] = maps[0]
    made = climb(nodes_low[below - dim :], nodes_high[below - dim :], maps[0], ids[pl.ds(position >> (level + 1), 1)])
    parts = []
    first = 0
    for k in range(1, level + 1):
        rows = dim << (level - k)
        parts += [nodes_low[first : first + rows], nodes_high[first : first + rows]]
        first += rows
    message[...] = jnp.concatenate(parts + [made] + maps[1:], axis=0)


def table_body(plan, n_chunks, dim, sizes, spot, *refs):
    chunks, (block, other, ids, out, message, matrix, held) = refs[:n_chunks], refs[n_chunks:]
    position, member = spot[0], spot[1]
    climb_stage(0, position, dim, sizes, block, other, ids, message, matrix)
    leaf_count, share = plan.leaf_count, plan.share
    held[...] = jnp.full(held.shape, -1, jnp.int32)

    def rows_of(start, count):
        return jnp.concatenate([chunk[pl.ds(start, count)] for chunk in chunks], axis=1)

    def split(entries, shift):
        tree = entries >> shift
        side = jnp.where(tree == position, 0, jnp.where(tree == (position ^ 1), 1, 2))
        return side, entries & ((1 << shift) - 1)

    slots = plan.slots
    entries = rows_of(member * share, share)
    side, within = split(entries, plan.levels)
    held[:share, :slots] = jnp.where(entries >= 0, side * leaf_count + within, -1)
    row = plan.far_row
    for degree in range(plan.levels + 1):
        count = plan.counts[degree]
        entries = rows_of(leaf_count + plan.first_rows[degree] + ((member * share) >> degree), count)
        side, within = split(entries, plan.levels - degree)
        held[row : row + count, :slots] = side * plan.per_side + plan.node_at(plan.first_rows[degree] + within)
        row += count
    at = leaf_count + plan.per_side - 1
    for level, count in enumerate(plan.upper_counts):
        entries = rows_of(at + (position >> (level + 1)), 1)
        held[row : row + 1, :slots] = entries + plan.upper_bases[level]
        row += 1
        at += count

    across = held[...].astype(F32).T
    square = (LANES, LANES)
    down_i = lax.broadcasted_iota(jnp.int32, square, 0)
    across_i = lax.broadcasted_iota(jnp.int32, square, 1)
    source = down_i.astype(F32)
    often = jnp.zeros(square, F32)
    for k in range(slots):
        often += jnp.where(across[k : k + 1] == source, 1.0, 0.0)
    near_r, far_r = plan.far_row, plan.upper_row
    half = jnp.where(across_i < near_r, leaf_count, plan.per_side)
    inside = down_i < 2 * half
    own = (inside & (across_i < far_r)) | ((across_i >= far_r) & (across_i < plan.rows))
    present = often > 0.0
    is_own = jnp.where(present & own, 1.0, 0.0)
    is_rim = jnp.where(present & jnp.logical_not(own), 1.0, 0.0)
    before = jnp.where(across_i < down_i, 1.0, 0.0).astype(BF)
    kind_down = (down_i >= near_r).astype(jnp.int32) + (down_i >= far_r).astype(jnp.int32)
    kind_across = (across_i >= near_r).astype(jnp.int32) + (across_i >= far_r).astype(jnp.int32)
    earlier = jnp.where((down_i < across_i) & (kind_down == kind_across), 1.0, 0.0).astype(BF)
    row_kind = kind_across[:1]
    lane = across_i[:1]
    totals = []
    rank = jnp.zeros(square, F32)
    for mask, starts in ((is_own, (0, 2, 4)), (is_rim, (1, 3, 4))):
        unit = jnp.where(row_kind == 0, float(NEAR_UNIT), float(FAR_UNIT))
        sums = jnp.sum(mask, axis=0, keepdims=True)
        sums = jnp.floor((sums + (unit - 1.0)) / unit) * unit
        base = nn(jnp.broadcast_to(sums, (16, LANES)).astype(BF), earlier)[:1]
        first = jnp.where(
            row_kind == 0,
            float(plan.starts[starts[0]]),
            jnp.where(row_kind == 1, float(plan.starts[starts[1]]), float(plan.starts[starts[2]])),
        )
        rank += mask * (nn(before, mask.astype(BF)) + base + first)
        for kind in range(3):
            totals.append(jnp.sum(jnp.where(row_kind == kind, sums, 0.0), axis=1, keepdims=True))
    spot_of = jnp.where(present & (across_i < plan.rows), rank, -1.0)
    spot_by_row = spot_of.T
    often_by_row = often.T
    part_rows = ceil_to(3 * plan.table_rows, 16)
    shape = (part_rows, LANES)
    part_i = lax.broadcasted_iota(jnp.int32, shape, 0)
    source_i = lax.broadcasted_iota(jnp.int32, shape, 1).astype(F32)
    part = (part_i >= plan.table_rows).astype(jnp.int32) + (part_i >= 2 * plan.table_rows).astype(jnp.int32)
    low = ((part_i - part * plan.table_rows) * LANES).astype(F32)
    slot_i = across_i.astype(F32)
    found = jnp.zeros(shape, F32)
    spot_low = spot_of - jnp.floor(spot_of * (1.0 / LANES)) * LANES
    spot_low = jnp.where(spot_of < 0.0, -1.0, spot_low)
    for r in range(plan.rows):
        where_to = spot_by_row[r : r + 1]
        value = jnp.where(part == 0, source_i, jnp.where(part == 1, often_by_row[r : r + 1], float(r)))
        value = jnp.where((where_to >= low) & (where_to < low + LANES), value, 0.0)
        hot = jnp.where(spot_low[:, r : r + 1] == slot_i, 1.0, 0.0).astype(BF)
        found += nn(value.astype(BF), hot)
    found = found.astype(jnp.int32)
    n = plan.table_rows
    out[:n] = found[:n] + found[n : 2 * n] * LANES + found[2 * n : 3 * n] * (LANES * 64)
    counts = jnp.zeros((1, LANES), F32)
    for at, total in enumerate((totals[0], totals[3], totals[1], totals[4], totals[2])):
        counts = jnp.where(lane == at, total, counts)
    out[n : n + 1] = counts.astype(jnp.int32)


def decode(table, at):
    code = table[at // LANES, at % LANES]
    return code & (LANES - 1), ((code >> 7) & 63).astype(F32), code >> 13


def add_items(plan, table, kind, sizes, goals, nodes, dim, scale, acc, first_row, first_source, half=None):
    unit, unroll = sizes
    depth = dim + NORM_ROWS
    start = plan.starts[kind]
    total = table[plan.table_rows, kind]
    group = unit * unroll

    def some(step, _):
        terms = []
        for k in range(unroll):
            items = [decode(table, start + step * group + k * unit + u) for u in range(unit)]
            sources = [jnp.maximum(item[0] - first_source, 0) for item in items]
            row = jnp.maximum(items[0][2] - first_row, 0)
            places = jnp.concatenate([nodes[source, :depth] for source in sources], axis=1)
            block = jnp.exp2(nn(goals[row], places) * scale)
            if unit > 1:
                width = block.shape[1] // unit
                block = jnp.concatenate(
                    [block[:, u * width : (u + 1) * width] * items[u][1] for u in range(unit)], axis=1
                )
            loads = jnp.concatenate([nodes[source, depth:] for source in sources], axis=1)
            term = nt(loads, block.astype(BF))
            terms.append((row, term if unit > 1 else term * items[0][1]))
        for row, term in terms:
            acc[row] += term
        return 0

    steps = (total + group - 1) // group
    first, last = {None: (0, steps), 0: (0, steps // 2), 1: (steps // 2, steps)}[half]
    lax.fori_loop(first, last, some, 0)


def leaf_copies(plan, bundle, leaves, at, dim, sems):
    some = slice(0, plan.leaf_count)
    there = pl.ds(at, plan.leaf_count)
    return [
        pltpu.make_async_copy(bundle.at[some, 0:dim], leaves.at[there, 0:dim], sems.at[0]),
        pltpu.make_async_copy(bundle.at[some, dim:], leaves.at[there, dim + NORM_ROWS :], sems.at[1]),
    ]


def node_copies(plan, bundle, nodes, at, dim, sems):
    count = plan.leaf_count
    skel = nodes.shape[2]
    copies = []
    for odd in range(2):
        there = pl.ds(at + odd * count, count)
        cols = slice(odd * skel, (odd + 1) * skel)
        copies += [
            pltpu.make_async_copy(bundle.at[count : 2 * count, 0:dim, cols], nodes.at[there, 0:dim], sems.at[2 * odd]),
            pltpu.make_async_copy(
                bundle.at[count : 2 * count, dim:, cols], nodes.at[there, dim + NORM_ROWS :], sems.at[2 * odd + 1]
            ),
        ]
    return copies


def run_copies(copies):
    for copy in copies:
        copy.start()
    for copy in copies:
        copy.wait()


def load_node(nodes, at, coords, loads, dim):
    nodes[at, :dim] = coords
    nodes[at, dim : dim + NORM_ROWS] = norm_rows(coords, 3)
    nodes[at, dim + NORM_ROWS :] = loads


def fill_norms(nodes, dim):
    for i in range(nodes.shape[0]):
        nodes[i, dim : dim + NORM_ROWS] = norm_rows(nodes[i, :dim], 3)


def near_body(plan, dim, sizes, scale, spot, table, bundle, pair, sent, other, ids, after, near, goals, leaves, message, matrix, sems):
    position, member = spot[0], spot[1]
    count, share = plan.leaf_count, plan.share
    copies = leaf_copies(plan, bundle, leaves, 0, dim, sems.at[0]) + leaf_copies(plan, pair, leaves, count, dim, sems.at[1])
    for copy in copies:
        copy.start()
    climb_stage(1, position, dim, sizes, sent, other, ids, message, matrix)
    for copy in copies:
        copy.wait()
    fill_norms(leaves, dim)
    for t in range(share):
        goals[t] = target_side(leaves[member * share + t, :dim])
    near[...] = jnp.zeros_like(near)
    add_items(plan, table, 0, NEAR_SIZES, goals, leaves, dim, scale, near, 0, 0, 0)


def near_rest_body(plan, dim, scale, table, near_in, goals, leaves, near):
    near[...] = near_in[...]
    add_items(plan, table, 0, NEAR_SIZES, goals, leaves, dim, scale, near, 0, 0, 1)


def far_body(plan, dim, scale, spot, table, bundle, pair, far, goals, passed, nodes, sems, pass_sem):
    move = pltpu.make_async_copy(bundle.at[0 : plan.leaf_count], passed, pass_sem)
    move.start()
    member = spot[1]
    run_copies(
        node_copies(plan, bundle, nodes, 0, dim, sems.at[0])
        + node_copies(plan, pair, nodes, plan.per_side, dim, sems.at[1])
    )
    fill_norms(nodes, dim)
    made = 0
    for degree in range(plan.levels + 1):
        start = plan.first_rows[degree] + ((member * plan.share) >> degree)
        for t in range(plan.counts[degree]):
            goals[made + t] = target_side(nodes[plan.node_at(start + t), :dim])
        made += plan.counts[degree]
    far[...] = jnp.zeros_like(far)
    add_items(plan, table, 2, FAR_SIZES, goals, nodes, dim, scale, far, plan.far_row, 0)
    move.wait()


def cross_far_body(plan, dim, map_sizes, scale, spot, table, cross, cross_leaves, far_in, goals, sent, other, upper_ids, after, far, message, matrix, nodes, places, index_sets, sems):
    count, skel, quarter = plan.leaf_count, nodes.shape[2], plan.leaf_count // 2
    rhs = nodes.shape[1] - dim - NORM_ROWS
    copies = [
        pltpu.make_async_copy(cross_leaves.at[0:count, 0:dim], places, sems.at[0]),
        pltpu.make_async_copy(cross.at[quarter, 0:count], index_sets, sems.at[1]),
    ]
    for odd in range(2):
        for half in range(2):
            first = odd * count + half * quarter
            copies.append(
                pltpu.make_async_copy(
                    cross.at[
                        0:quarter, half * rhs : (half + 1) * rhs, odd * skel : (odd + 1) * skel
                    ],
                    nodes.at[first : first + quarter, dim + NORM_ROWS :],
                    sems.at[2 + 2 * odd + half],
                )
            )
    for copy in copies:
        copy.start()
    climb_stage(2, spot[0], dim, map_sizes, sent, other, upper_ids, message, matrix)
    for copy in copies:
        copy.wait()
    ids = index_sets[...].astype(F32).astype(jnp.int32)
    for i in range(count):
        nodes[plan.node_at(i), :dim] = pick(places[i], ids[i : i + 1, :skel])
    row = 0
    for degree in range(1, plan.levels + 1):
        for i in range(count >> degree):
            below = plan.first_rows[degree - 1] + 2 * i
            both = jnp.concatenate(
                [nodes[plan.node_at(below), :dim], nodes[plan.node_at(below + 1), :dim]], axis=1
            )
            nodes[plan.node_at(plan.first_rows[degree] + i), :dim] = pick(both, ids[row : row + 1, skel:])
            row += 1
    nodes[2 * count - 1, :dim] = jnp.zeros((dim, skel), BF)
    fill_norms(nodes, dim)
    far[...] = far_in[...]
    add_items(plan, table, 3, FAR_SIZES, goals, nodes, dim, scale, far, plan.far_row, 2 * plan.per_side)


def cross_near_body(plan, dim, scale, table, cross, near_in, goals, after, near, leaves, sems):
    run_copies(leaf_copies(plan, cross, leaves, 0, dim, sems))
    fill_norms(leaves, dim)
    near[...] = near_in[...]
    add_items(plan, table, 1, NEAR_SIZES, goals, leaves, dim, scale, near, 0, 2 * plan.leaf_count)


def down_body(plan, dim, scale, spot, table, *refs):
    n_pieces = plan.upper_counts[-1]
    pieces, refs = refs[:n_pieces], refs[n_pieces:]
    matrices, (far, near, inner_maps, leaf_maps, out, nodes, goals, acc) = refs[:3], refs[3:]
    leaf_count, skel, leaf_size = leaf_maps.shape
    share, levels = plan.share, plan.levels
    depth = dim + NORM_ROWS
    position, member = spot[0], spot[1]

    top = len(plan.upper_counts)
    for k, piece in enumerate(pieces):
        group = (position >> top) ^ k
        row = 0
        for level in range(top):
            each = 1 << (top - 1 - level)
            for i in range(each):
                node = piece[row : row + dim]
                load_node(nodes, plan.upper_bases[level] + group * each + i, node[:, :skel], node[:, skel:], dim)
                row += dim

    for level in range(len(plan.upper_counts)):
        goals[level] = target_side(nodes[plan.upper_bases[level] + (position >> (level + 1)), :dim])
    acc[...] = jnp.zeros_like(acc)
    add_items(plan, table, 4, FAR_SIZES, goals, nodes, dim, scale, acc, plan.upper_row, 0)

    total = None
    for level in range(len(plan.upper_counts) - 1, -1, -1):
        total = acc[level] if total is None else total + acc[level]
        branch = (position >> level) & 1
        cols = pl.ds(pl.multiple_of(branch * skel, skel), skel)
        matrix = matrices[level][:, cols]
        total = through(total, matrix)

    firsts = []
    made = 0
    for degree in range(levels + 1):
        firsts.append(made)
        made += max(1, share >> degree)
    totals = [total + far[firsts[levels]]]
    for degree in range(levels, 0, -1):
        first_row = leaf_count - 2 * (leaf_count >> degree)
        start = (member * share) >> degree
        child_start = (member * share) >> (degree - 1)
        children = max(1, share >> (degree - 1))
        after = []
        if children == 1:
            branch = child_start & 1
            cols = pl.ds(pl.multiple_of(branch * skel, skel), skel)
            after.append(through(totals[0], inner_maps[first_row + start, :, cols]) + far[firsts[degree - 1]])
        else:
            for c in range(children // 2):
                both = through(totals[c], inner_maps[first_row + start + c])
                after.append(both[:, :skel] + far[firsts[degree - 1] + 2 * c])
                after.append(both[:, skel:] + far[firsts[degree - 1] + 2 * c + 1])
        totals = after
    for c in range(share):
        out[:, c * leaf_size : (c + 1) * leaf_size] = (
            through(totals[c], leaf_maps[member * share + c]) + near[c]
        )


def on_device(
    points,
    charges,
    leaf_ids,
    inner_ids,
    upper_ids_first,
    upper_ids_second,
    upper_ids_third,
    leaf_maps,
    inner_maps,
    upper_maps_first,
    upper_maps_second,
    upper_maps_third,
    near_lists,
    far_inner,
    far_upper_first,
    far_upper_second,
    far_upper_third,
):
    dim, local_points = points.shape
    rhs = charges.shape[0]
    leaf_count, skel, leaf_size = leaf_maps.shape
    levels = leaf_count.bit_length() - 1
    stacked = dim + rhs
    depth = dim + NORM_ROWS
    subtrees = lax.axis_size("leaf")
    list_size = lax.axis_size("list")
    share = leaf_count // list_size
    scale = -3.0 / dim * math.log2(math.e)
    on_chip = [(i, i ^ 1) for i in range(subtrees)]
    across = [pair for i in range(1, subtrees - 1, 2) for pair in ((i, i + 1), (i + 1, i))]

    spot = jnp.stack([lax.axis_index("leaf"), lax.axis_index("list")]).astype(jnp.int32)
    mine = jnp.concatenate(
        [near_lists, far_inner, far_upper_first, far_upper_second, far_upper_third], axis=0
    )
    chunks = [mine] + [
        lax.ppermute(mine, "list", [(i, (i + shift) % list_size) for i in range(list_size)])
        for shift in range(1, list_size)
    ]
    uppers = (far_upper_first, far_upper_second, far_upper_third)
    plan = Plan(leaf_count, share, levels, list_size * mine.shape[1], [a.shape[0] for a in uppers])

    vmem = pl.BlockSpec(memory_space=pltpu.VMEM)
    smem = pl.BlockSpec(memory_space=pltpu.SMEM)
    anywhere = pl.BlockSpec(memory_space=pl.ANY)
    params = pltpu.CompilerParams(vmem_limit_bytes=VMEM_BYTES)

    def shaped(shape, dtype=BF):
        return jax.ShapeDtypeStruct(shape, dtype)

    def cost(flops, transcendentals=0):
        return pl.CostEstimate(flops=flops, bytes_accessed=4 * 10**6, transcendentals=transcendentals)

    inputs = (points, charges, leaf_ids, inner_ids, leaf_maps, inner_maps, upper_maps_first, upper_maps_second, upper_maps_third)
    block_rows = dim + sum(a.shape[0] for a in inputs[6:])
    bundle, extras, block = pl.pallas_call(
        functools.partial(up_body, levels),
        out_shape=(shaped((2 * leaf_count, stacked, leaf_size)), shaped((leaf_count // 2 + 1, stacked, leaf_size)), shaped((block_rows, 2 * skel))),
        in_specs=[anywhere] * 9,
        out_specs=(vmem, vmem, vmem),
        scratch_shapes=[pltpu.VMEM(a.shape, a.dtype) for a in inputs] + [pltpu.SemaphoreType.DMA((9,))],
        compiler_params=pltpu.CompilerParams(vmem_limit_bytes=UP_VMEM_BYTES),
        name="upward",
        cost_estimate=cost(10**11),
    )(*inputs)

    cross = lax.ppermute(extras, "leaf", across)
    pair = lax.ppermute(bundle, "leaf", on_chip)
    def swapped(value, mask):
        return lax.ppermute(value, "leaf", [(i, i ^ mask) for i in range(subtrees)])

    sizes = [a.shape[0] for a in inputs[6:]]
    matrix_shape = shaped((skel, 2 * skel))

    def message_shape(level):
        rows = sum(dim << (level - k) for k in range(level + 1)) + sum(rows << (level + 1) for rows in sizes[level + 1 :])
        return shaped((rows, 2 * skel))

    table, first_message, first_matrix = pl.pallas_call(
        functools.partial(table_body, plan, len(chunks), dim, sizes),
        out_shape=(shaped((plan.out_rows, LANES), jnp.int32), message_shape(0), matrix_shape),
        in_specs=[smem] + [vmem] * (len(chunks) + 3),
        out_specs=(vmem,) * 3,
        scratch_shapes=[pltpu.VMEM((LANES, LANES), jnp.int32)],
        compiler_params=params,
        name="table",
        cost_estimate=cost(10**9),
    )(spot, *chunks, block, swapped(block, 1), upper_ids_first)

    acc_shapes = (shaped((share, rhs, leaf_size), F32), shaped((plan.targets, rhs, skel), F32))
    goal_shapes = (shaped((share, leaf_size, depth)), shaped((plan.targets, skel, depth)))

    def nodes_of(sides):
        return pltpu.VMEM((sides * plan.per_side, depth + rhs, skel), BF)

    far, far_goals, passed = pl.pallas_call(
        functools.partial(far_body, plan, dim, scale),
        out_shape=(acc_shapes[1], goal_shapes[1], shaped((leaf_count, stacked, leaf_size))),
        in_specs=[smem, smem, anywhere, anywhere],
        out_specs=(vmem, vmem, anywhere),
        scratch_shapes=[nodes_of(2), pltpu.SemaphoreType.DMA((2, 4)), pltpu.SemaphoreType.DMA],
        compiler_params=params,
        name="far",
        cost_estimate=cost(10**10, 10**7),
    )(spot, table, bundle, pair)
    cross_leaves = lax.ppermute(passed, "leaf", across)

    leaves_shape = shaped((2 * leaf_count, depth + rhs, leaf_size))
    near, near_goals, leaves, second_message, second_matrix = pl.pallas_call(
        functools.partial(near_body, plan, dim, sizes, scale),
        out_shape=(acc_shapes[0], goal_shapes[0], leaves_shape, message_shape(1), matrix_shape),
        in_specs=[smem, smem] + [anywhere] * 2 + [vmem] * 3 + [anywhere],
        out_specs=(vmem,) * 5,
        scratch_shapes=[pltpu.SemaphoreType.DMA((2, 2))],
        compiler_params=params,
        name="near",
        cost_estimate=cost(10**10, 10**7),
    )(spot, table, bundle, pair, first_message, swapped(first_message, 2), upper_ids_second, far)

    near = pl.pallas_call(
        functools.partial(near_rest_body, plan, dim, scale),
        out_shape=acc_shapes[0],
        in_specs=[smem] + [vmem] * 3,
        out_specs=vmem,
        compiler_params=params,
        name="nearrest",
        cost_estimate=cost(10**7),
    )(table, near, near_goals, leaves)

    far, third_message, third_matrix = pl.pallas_call(
        functools.partial(cross_far_body, plan, dim, sizes, scale),
        out_shape=(acc_shapes[1], message_shape(2), matrix_shape),
        in_specs=[smem, smem, anywhere, anywhere] + [vmem] * 5 + [anywhere],
        out_specs=(vmem,) * 3,
        scratch_shapes=[
            nodes_of(1),
            pltpu.VMEM((leaf_count, dim, leaf_size), BF),
            pltpu.VMEM((leaf_count, leaf_size), BF),
            pltpu.SemaphoreType.DMA((6,)),
        ],
        compiler_params=params,
        name="crossfar",
        cost_estimate=cost(10**10, 10**7),
    )(spot, table, cross, cross_leaves, far, far_goals, second_message, swapped(second_message, 4), upper_ids_third, near)

    pieces = [third_message] + [swapped(third_message, mask) for mask in range(8, subtrees, 8)]

    near = pl.pallas_call(
        functools.partial(cross_near_body, plan, dim, scale),
        out_shape=acc_shapes[0],
        in_specs=[smem, anywhere, vmem, vmem, anywhere],
        out_specs=vmem,
        scratch_shapes=[pltpu.VMEM((leaf_count, depth + rhs, leaf_size), BF), pltpu.SemaphoreType.DMA((2,))],
        compiler_params=params,
        name="crossnear",
        cost_estimate=cost(10**10, 10**7),
    )(table, cross_leaves, near, near_goals, far)

    return pl.pallas_call(
        functools.partial(down_body, plan, dim, scale),
        out_shape=shaped((rhs, share * leaf_size), F32),
        in_specs=[smem, smem] + [vmem] * (len(pieces) + 7),
        out_specs=vmem,
        scratch_shapes=[
            pltpu.VMEM((sum(plan.upper_counts), depth + rhs, skel), BF),
            pltpu.VMEM((len(uppers), skel, depth), BF),
            pltpu.VMEM((len(uppers), rhs, skel), F32),
        ],
        compiler_params=params,
        name="down",
        cost_estimate=cost(10**9, 10**6),
    )(spot, table, *pieces, first_matrix, second_matrix, third_matrix, far, near, inner_maps, leaf_maps)


def solution(mesh):
    placed = (
        P(None, "leaf"),
        P(None, "leaf"),
        P("leaf", None),
        P("leaf", None),
        P(),
        P(),
        P(),
        P("leaf", None, None),
        P("leaf", None, None),
        P("leaf", None),
        P("leaf", None),
        P("leaf", None),
        P("leaf", "list"),
        P("leaf", "list"),
        P(None, "list"),
        P(None, "list"),
        P(None, "list"),
    )
    return jax.shard_map(
        on_device, mesh=mesh, in_specs=placed, out_specs=P(None, ("leaf", "list")), check_vma=False
    )
```

```python
import functools
import math

import jax
import jax.numpy as jnp
from jax import lax
from jax.experimental import pallas as pl
from jax.experimental.pallas import tpu as pltpu
from jax.sharding import PartitionSpec as P

BF = jnp.bfloat16
F32 = jnp.float32
NORM_ROWS = 16
VMEM_BYTES = 40 * 2**20
UP_VMEM_BYTES = 60 * 2**20
LANES = 128
NEAR_UNIT = 1
FAR_UNIT = 2
NEAR_SIZES = (NEAR_UNIT, 16)
FAR_SIZES = (FAR_UNIT, 16)


def nt(a, b):
    return lax.dot_general(a, b, (((1,), (1,)), ((), ())), preferred_element_type=F32)


def nn(a, b):
    return jnp.dot(a, b, preferred_element_type=F32)


def pick(coords, ids):
    shape = (coords.shape[1], ids.shape[1])
    hot = (lax.broadcasted_iota(jnp.int32, shape, 0) == ids).astype(BF)
    return nn(coords, hot).astype(BF)


def norm_rows(coords, first):
    wide = coords.astype(F32)
    norm = jnp.sum(wide * wide, axis=0, keepdims=True)
    high = norm.astype(BF).astype(F32)
    rest = norm - high
    middle = rest.astype(BF).astype(F32)
    low = rest - middle
    row = lax.broadcasted_iota(jnp.int32, (NORM_ROWS, coords.shape[1]), 0)
    parts = jnp.where(row == first, high, jnp.where(row == first + 1, middle, low))
    inside = (row >= first) & (row < first + 3)
    ones = (row < 6) & jnp.logical_not(inside)
    return jnp.where(inside, parts, jnp.where(ones, 1.0, 0.0)).astype(BF)


def target_side(coords):
    rows = jnp.concatenate(
        [coords.astype(F32) * -2.0, norm_rows(coords, 0).astype(F32)], axis=0
    )
    depth, count = rows.shape
    padded = jnp.concatenate([rows, jnp.zeros((128 - depth, count), F32)], axis=0)
    return padded.T.astype(BF)[:, :depth]


def kernel_block(goal, source, scale):
    return jnp.exp2(nn(goal, source) * scale).astype(BF)


def halves(value):
    high = value.astype(BF)
    low = (value - high.astype(F32)).astype(BF)
    return jnp.concatenate([high, low], axis=0)


def through(value, matrix):
    count = value.shape[0]
    both = nn(halves(value), matrix)
    return both[:count] + both[count:]


def up_body(levels, *refs):
    sources, (bundle, extras, block), held, sems = refs[:9], refs[9:12], refs[12:21], refs[21]
    copies = [pltpu.make_async_copy(src, dst, sems.at[i]) for i, (src, dst) in enumerate(zip(sources, held))]
    for copy in copies:
        copy.start()
    points, charges, leaf_ids, inner_ids, leaf_maps, inner_maps = held[:6]
    leaf_count, skel, leaf_size = leaf_maps.shape
    dim = points.shape[0]
    quarter = leaf_count // 2

    def put(node, place, load):
        cols = slice((node % 2) * skel, (node % 2 + 1) * skel)
        bundle[leaf_count + node // 2, :dim, cols] = place
        bundle[leaf_count + node // 2, dim:, cols] = load
        rhs = load.shape[0]
        pair, half = node // 2 % quarter, node // 2 // quarter
        extras[pair, half * rhs : (half + 1) * rhs, cols] = load

    for i in (0, 2):
        copies[i].wait()
    places = []
    for i in range(leaf_count):
        mine = points[:, i * leaf_size : (i + 1) * leaf_size]
        bundle[i, :dim] = mine
        places.append(pick(mine, leaf_ids[i : i + 1]))
    for i in (1, 4):
        copies[i].wait()
    for i in range(leaf_count):
        mine = charges[:, i * leaf_size : (i + 1) * leaf_size]
        bundle[i, dim:] = mine
        put(i, places[i], nt(mine, leaf_maps[i]).astype(BF))
    for i in (3, 5):
        copies[i].wait()
    extras[quarter] = jnp.zeros(extras.shape[1:], BF)
    extras[quarter, :leaf_count, :skel] = leaf_ids[...].astype(F32).astype(BF)
    extras[quarter, :leaf_count, skel:] = jnp.concatenate(
        [inner_ids[...], jnp.zeros((1, skel), jnp.int32)], axis=0
    ).astype(F32).astype(BF)
    below, here, row = 0, leaf_count, 0
    for degree in range(1, levels + 1):
        for i in range(leaf_count >> degree):
            pair = bundle[leaf_count + below // 2 + i]
            put(here + i, pick(pair[:dim], inner_ids[row : row + 1]), nt(pair[dim:], inner_maps[row]).astype(BF))
            row += 1
        below = here
        here += leaf_count >> degree
    for node in range(here, 2 * leaf_count):
        empty = jnp.zeros((dim, skel), BF)
        put(node, empty, jnp.zeros((bundle.shape[1] - dim, skel), BF))
    last = here - 1
    root = bundle[leaf_count + last // 2, :, (last % 2) * skel : (last % 2 + 1) * skel]
    parts = [jnp.concatenate([root[:dim], root[dim:]], axis=1)]
    for i in (6, 7, 8):
        copies[i].wait()
        parts.append(held[i][...])
    whole = jnp.concatenate(parts, axis=0)
    block[...] = whole


def ceil_to(value, unit):
    return -(-value // unit) * unit


class Plan:
    def __init__(self, leaf_count, share, levels, slots, upper_counts):
        self.leaf_count, self.share, self.levels, self.slots = leaf_count, share, levels, slots
        self.per_side = 2 * leaf_count
        self.counts = [max(1, share >> degree) for degree in range(levels + 1)]
        self.first_rows = [2 * leaf_count - 2 * (leaf_count >> degree) for degree in range(levels + 1)]
        self.targets = sum(self.counts)
        self.far_row = share
        self.upper_row = share + self.targets
        self.rows = self.upper_row + len(upper_counts)
        self.upper_counts = upper_counts
        self.upper_bases = [sum(upper_counts[:i]) for i in range(len(upper_counts))]
        trees = [leaf_count >> degree for degree in range(levels + 1)]
        def room(count, unit):
            return ceil_to(min(slots, count), unit)

        most = [
            share * room(2 * leaf_count, NEAR_UNIT),
            share * room(leaf_count, NEAR_UNIT),
            sum(c * room(2 * t, FAR_UNIT) for c, t in zip(self.counts, trees)),
            sum(c * room(t, FAR_UNIT) for c, t in zip(self.counts, trees)),
            sum(room(c, FAR_UNIT) for c in upper_counts),
        ]
        self.starts, at = [], 0
        for count in most:
            self.starts.append(at)
            at += ceil_to(count, LANES)
        self.table_rows = at // LANES
        self.out_rows = ceil_to(self.table_rows + 1, 8)
        width = max(3 * leaf_count, 3 * self.per_side, sum(upper_counts))
        assert width <= LANES and self.rows <= LANES and slots <= LANES

    def node_at(self, node):
        return (node & 1) * self.leaf_count + (node >> 1)


def in_order(bit, mine, theirs):
    low = jnp.where(bit == 0, mine, theirs)
    high = jnp.where(bit == 0, theirs, mine)
    return low, high


def climb(low, high, matrix, ids):
    skel = low.shape[1] // 2
    coords = jnp.concatenate([low[:, :skel], high[:, :skel]], axis=1)
    loads = jnp.concatenate([low[:, skel:], high[:, skel:]], axis=1)
    return jnp.concatenate([pick(coords, ids), nt(loads, matrix).astype(BF)], axis=1)


def climb_stage(level, position, dim, sizes, mine, theirs, ids, message, matrix_out):
    bit = (position >> level) & 1
    low, high = in_order(bit, mine[...], theirs[...])
    below = sum(dim << (level - k) for k in range(1, level + 1)) if level else dim
    nodes_low, nodes_high = low[:below], high[:below]
    at = below
    maps = []
    for rows in sizes[level:]:
        rows = rows << level
        maps.append(jnp.concatenate([low[at : at + rows], high[at : at + rows]], axis=0))
        at += rows
    matrix_out[...] = maps[0]
    made = climb(nodes_low[below - dim :], nodes_high[below - dim :], maps[0], ids[pl.ds(position >> (level + 1), 1)])
    parts = []
    first = 0
    for k in range(1, level + 1):
        rows = dim << (level - k)
        parts += [nodes_low[first : first + rows], nodes_high[first : first + rows]]
        first += rows
    message[...] = jnp.concatenate(parts + [made] + maps[1:], axis=0)


def table_body(plan, n_chunks, dim, sizes, spot, *refs):
    chunks, (block, other, ids, bundle, extras, out, message, matrix, slim, held, blocks, sems) = refs[:n_chunks], refs[n_chunks:]
    count = plan.leaf_count
    moves = [
        pltpu.make_async_copy(bundle.at[0:count], slim.at[0:count], sems.at[0]),
        pltpu.make_async_copy(extras, slim.at[count:], sems.at[1]),
    ]
    inputs = [
        pltpu.make_async_copy(block, blocks.at[0], sems.at[2]),
        pltpu.make_async_copy(other, blocks.at[1], sems.at[3]),
    ]
    for move in inputs + moves:
        move.start()
    position, member = spot[0], spot[1]
    leaf_count, share = plan.leaf_count, plan.share
    held[...] = jnp.full(held.shape, -1, jnp.int32)

    def rows_of(start, count):
        return jnp.concatenate([chunk[pl.ds(start, count)] for chunk in chunks], axis=1)

    def split(entries, shift):
        tree = entries >> shift
        side = jnp.where(tree == position, 0, jnp.where(tree == (position ^ 1), 1, 2))
        return side, entries & ((1 << shift) - 1)

    slots = plan.slots
    entries = rows_of(member * share, share)
    side, within = split(entries, plan.levels)
    held[:share, :slots] = jnp.where(entries >= 0, side * leaf_count + within, -1)
    row = plan.far_row
    for degree in range(plan.levels + 1):
        count = plan.counts[degree]
        entries = rows_of(leaf_count + plan.first_rows[degree] + ((member * share) >> degree), count)
        side, within = split(entries, plan.levels - degree)
        held[row : row + count, :slots] = side * plan.per_side + plan.node_at(plan.first_rows[degree] + within)
        row += count
    at = leaf_count + plan.per_side - 1
    for level, count in enumerate(plan.upper_counts):
        entries = rows_of(at + (position >> (level + 1)), 1)
        held[row : row + 1, :slots] = entries + plan.upper_bases[level]
        row += 1
        at += count

    across = held[...].astype(F32).T
    square = (LANES, LANES)
    down_i = lax.broadcasted_iota(jnp.int32, square, 0)
    across_i = lax.broadcasted_iota(jnp.int32, square, 1)
    source = down_i.astype(F32)
    often = jnp.zeros(square, F32)
    for k in range(slots):
        often += jnp.where(across[k : k + 1] == source, 1.0, 0.0)
    near_r, far_r = plan.far_row, plan.upper_row
    half = jnp.where(across_i < near_r, leaf_count, plan.per_side)
    inside = down_i < 2 * half
    own = (inside & (across_i < far_r)) | ((across_i >= far_r) & (across_i < plan.rows))
    present = often > 0.0
    is_own = jnp.where(present & own, 1.0, 0.0)
    is_rim = jnp.where(present & jnp.logical_not(own), 1.0, 0.0)
    before = jnp.where(across_i < down_i, 1.0, 0.0).astype(BF)
    kind_down = (down_i >= near_r).astype(jnp.int32) + (down_i >= far_r).astype(jnp.int32)
    kind_across = (across_i >= near_r).astype(jnp.int32) + (across_i >= far_r).astype(jnp.int32)
    earlier = jnp.where((down_i < across_i) & (kind_down == kind_across), 1.0, 0.0).astype(BF)
    row_kind = kind_across[:1]
    lane = across_i[:1]
    totals = []
    rank = jnp.zeros(square, F32)
    for mask, starts in ((is_own, (0, 2, 4)), (is_rim, (1, 3, 4))):
        unit = jnp.where(row_kind == 0, float(NEAR_UNIT), float(FAR_UNIT))
        sums = jnp.sum(mask, axis=0, keepdims=True)
        sums = jnp.floor((sums + (unit - 1.0)) / unit) * unit
        base = nn(jnp.broadcast_to(sums, (16, LANES)).astype(BF), earlier)[:1]
        first = jnp.where(
            row_kind == 0,
            float(plan.starts[starts[0]]),
            jnp.where(row_kind == 1, float(plan.starts[starts[1]]), float(plan.starts[starts[2]])),
        )
        rank += mask * (nn(before, mask.astype(BF)) + base + first)
        for kind in range(3):
            totals.append(jnp.sum(jnp.where(row_kind == kind, sums, 0.0), axis=1, keepdims=True))
    spot_of = jnp.where(present & (across_i < plan.rows), rank, -1.0)
    spot_by_row = spot_of.T
    often_by_row = often.T
    part_rows = ceil_to(3 * plan.table_rows, 16)
    shape = (part_rows, LANES)
    part_i = lax.broadcasted_iota(jnp.int32, shape, 0)
    source_i = lax.broadcasted_iota(jnp.int32, shape, 1).astype(F32)
    part = (part_i >= plan.table_rows).astype(jnp.int32) + (part_i >= 2 * plan.table_rows).astype(jnp.int32)
    low = ((part_i - part * plan.table_rows) * LANES).astype(F32)
    slot_i = across_i.astype(F32)
    found = jnp.zeros(shape, F32)
    spot_low = spot_of - jnp.floor(spot_of * (1.0 / LANES)) * LANES
    spot_low = jnp.where(spot_of < 0.0, -1.0, spot_low)
    for r in range(plan.rows):
        where_to = spot_by_row[r : r + 1]
        value = jnp.where(part == 0, source_i, jnp.where(part == 1, often_by_row[r : r + 1], float(r)))
        value = jnp.where((where_to >= low) & (where_to < low + LANES), value, 0.0)
        hot = jnp.where(spot_low[:, r : r + 1] == slot_i, 1.0, 0.0).astype(BF)
        found += nn(value.astype(BF), hot)
    found = found.astype(jnp.int32)
    n = plan.table_rows
    out[:n] = found[:n] + found[n : 2 * n] * LANES + found[2 * n : 3 * n] * (LANES * 64)
    counts = jnp.zeros((1, LANES), F32)
    for at, total in enumerate((totals[0], totals[3], totals[1], totals[4], totals[2])):
        counts = jnp.where(lane == at, total, counts)
    out[n : n + 1] = counts.astype(jnp.int32)
    for move in inputs:
        move.wait()
    climb_stage(0, position, dim, sizes, blocks.at[0], blocks.at[1], ids, message, matrix)
    for move in moves:
        move.wait()


def decode(table, at):
    code = table[at // LANES, at % LANES]
    return code & (LANES - 1), ((code >> 7) & 63).astype(F32), code >> 13


def add_items(plan, table, kind, sizes, goals, nodes, dim, scale, acc, first_row, first_source, half=None):
    unit, unroll = sizes
    depth = dim + NORM_ROWS
    start = plan.starts[kind]
    total = table[plan.table_rows, kind]
    group = unit * unroll

    def some(step, _):
        terms = []
        for k in range(unroll):
            items = [decode(table, start + step * group + k * unit + u) for u in range(unit)]
            sources = [jnp.maximum(item[0] - first_source, 0) for item in items]
            row = jnp.maximum(items[0][2] - first_row, 0)
            places = jnp.concatenate([nodes[source, :depth] for source in sources], axis=1)
            block = jnp.exp2(nn(goals[row], places) * scale)
            if unit > 1:
                width = block.shape[1] // unit
                block = jnp.concatenate(
                    [block[:, u * width : (u + 1) * width] * items[u][1] for u in range(unit)], axis=1
                )
            loads = jnp.concatenate([nodes[source, depth:] for source in sources], axis=1)
            term = nt(loads, block.astype(BF))
            terms.append((row, term if unit > 1 else term * items[0][1]))
        for row, term in terms:
            acc[row] += term
        return 0

    steps = (total + group - 1) // group
    first, last = {None: (0, steps), 0: (0, steps // 2), 1: (steps // 2, steps)}[half]
    lax.fori_loop(first, last, some, 0)


def leaf_copies(plan, bundle, leaves, at, dim, sems):
    some = slice(0, plan.leaf_count)
    there = pl.ds(at, plan.leaf_count)
    return [
        pltpu.make_async_copy(bundle.at[some, 0:dim], leaves.at[there, 0:dim], sems.at[0]),
        pltpu.make_async_copy(bundle.at[some, dim:], leaves.at[there, dim + NORM_ROWS :], sems.at[1]),
    ]


def node_copies(plan, bundle, nodes, at, dim, sems):
    count = plan.leaf_count
    skel = nodes.shape[2]
    copies = []
    for odd in range(2):
        there = pl.ds(at + odd * count, count)
        cols = slice(odd * skel, (odd + 1) * skel)
        copies += [
            pltpu.make_async_copy(bundle.at[count : 2 * count, 0:dim, cols], nodes.at[there, 0:dim], sems.at[2 * odd]),
            pltpu.make_async_copy(
                bundle.at[count : 2 * count, dim:, cols], nodes.at[there, dim + NORM_ROWS :], sems.at[2 * odd + 1]
            ),
        ]
    return copies


def run_copies(copies):
    for copy in copies:
        copy.start()
    for copy in copies:
        copy.wait()


def load_node(nodes, at, coords, loads, dim):
    nodes[at, :dim] = coords
    nodes[at, dim : dim + NORM_ROWS] = norm_rows(coords, 3)
    nodes[at, dim + NORM_ROWS :] = loads


def fill_norms(nodes, dim):
    for i in range(nodes.shape[0]):
        nodes[i, dim : dim + NORM_ROWS] = norm_rows(nodes[i, :dim], 3)


def near_body(plan, dim, sizes, scale, spot, table, bundle, pair, sent, other, ids, after, near, goals, leaves, message, matrix, sems):
    position, member = spot[0], spot[1]
    count, share = plan.leaf_count, plan.share
    copies = leaf_copies(plan, bundle, leaves, 0, dim, sems.at[0]) + leaf_copies(plan, pair, leaves, count, dim, sems.at[1])
    for copy in copies:
        copy.start()
    climb_stage(1, position, dim, sizes, sent, other, ids, message, matrix)
    for copy in copies:
        copy.wait()
    fill_norms(leaves, dim)
    for t in range(share):
        goals[t] = target_side(leaves[member * share + t, :dim])
    near[...] = jnp.zeros_like(near)
    add_items(plan, table, 0, NEAR_SIZES, goals, leaves, dim, scale, near, 0, 0, 0)


def near_rest_body(plan, dim, scale, table, near_in, goals, leaves, near):
    near[...] = near_in[...]
    add_items(plan, table, 0, NEAR_SIZES, goals, leaves, dim, scale, near, 0, 0, 1)


def far_body(plan, dim, scale, spot, table, bundle, pair, far, goals, nodes, sems):
    member = spot[1]
    run_copies(
        node_copies(plan, bundle, nodes, 0, dim, sems.at[0])
        + node_copies(plan, pair, nodes, plan.per_side, dim, sems.at[1])
    )
    fill_norms(nodes, dim)
    made = 0
    for degree in range(plan.levels + 1):
        start = plan.first_rows[degree] + ((member * plan.share) >> degree)
        for t in range(plan.counts[degree]):
            goals[made + t] = target_side(nodes[plan.node_at(start + t), :dim])
        made += plan.counts[degree]
    far[...] = jnp.zeros_like(far)
    add_items(plan, table, 2, FAR_SIZES, goals, nodes, dim, scale, far, plan.far_row, 0)


def cross_far_body(plan, dim, map_sizes, scale, spot, table, cross, far_in, goals, sent, other, upper_ids, after, far, message, matrix, nodes, places, index_sets, sems):
    count, skel, quarter = plan.leaf_count, nodes.shape[2], plan.leaf_count // 2
    rhs = nodes.shape[1] - dim - NORM_ROWS
    copies = [
        pltpu.make_async_copy(cross.at[0:count, 0:dim], places, sems.at[0]),
        pltpu.make_async_copy(cross.at[count + quarter, 0:count], index_sets, sems.at[1]),
    ]
    for odd in range(2):
        for half in range(2):
            first = odd * count + half * quarter
            copies.append(
                pltpu.make_async_copy(
                    cross.at[
                        count : count + quarter, half * rhs : (half + 1) * rhs, odd * skel : (odd + 1) * skel
                    ],
                    nodes.at[first : first + quarter, dim + NORM_ROWS :],
                    sems.at[2 + 2 * odd + half],
                )
            )
    for copy in copies:
        copy.start()
    climb_stage(2, spot[0], dim, map_sizes, sent, other, upper_ids, message, matrix)
    for copy in copies:
        copy.wait()
    ids = index_sets[...].astype(F32).astype(jnp.int32)
    for i in range(count):
        nodes[plan.node_at(i), :dim] = pick(places[i], ids[i : i + 1, :skel])
    row = 0
    for degree in range(1, plan.levels + 1):
        for i in range(count >> degree):
            below = plan.first_rows[degree - 1] + 2 * i
            both = jnp.concatenate(
                [nodes[plan.node_at(below), :dim], nodes[plan.node_at(below + 1), :dim]], axis=1
            )
            nodes[plan.node_at(plan.first_rows[degree] + i), :dim] = pick(both, ids[row : row + 1, skel:])
            row += 1
    nodes[2 * count - 1, :dim] = jnp.zeros((dim, skel), BF)
    fill_norms(nodes, dim)
    far[...] = far_in[...]
    add_items(plan, table, 3, FAR_SIZES, goals, nodes, dim, scale, far, plan.far_row, 2 * plan.per_side)


def cross_near_body(plan, dim, scale, table, cross, near_in, goals, after, near, leaves, sems):
    run_copies(leaf_copies(plan, cross, leaves, 0, dim, sems))
    fill_norms(leaves, dim)
    near[...] = near_in[...]
    add_items(plan, table, 1, NEAR_SIZES, goals, leaves, dim, scale, near, 0, 2 * plan.leaf_count)


def down_body(plan, dim, scale, spot, table, *refs):
    n_pieces = plan.upper_counts[-1]
    pieces, refs = refs[:n_pieces], refs[n_pieces:]
    matrices, (far, near, inner_maps, leaf_maps, out, nodes, goals, acc) = refs[:3], refs[3:]
    leaf_count, skel, leaf_size = leaf_maps.shape
    share, levels = plan.share, plan.levels
    depth = dim + NORM_ROWS
    position, member = spot[0], spot[1]

    top = len(plan.upper_counts)
    for k, piece in enumerate(pieces):
        group = (position >> top) ^ k
        row = 0
        for level in range(top):
            each = 1 << (top - 1 - level)
            for i in range(each):
                node = piece[row : row + dim]
                load_node(nodes, plan.upper_bases[level] + group * each + i, node[:, :skel], node[:, skel:], dim)
                row += dim

    for level in range(len(plan.upper_counts)):
        goals[level] = target_side(nodes[plan.upper_bases[level] + (position >> (level + 1)), :dim])
    acc[...] = jnp.zeros_like(acc)
    add_items(plan, table, 4, FAR_SIZES, goals, nodes, dim, scale, acc, plan.upper_row, 0)

    total = None
    for level in range(len(plan.upper_counts) - 1, -1, -1):
        total = acc[level] if total is None else total + acc[level]
        branch = (position >> level) & 1
        cols = pl.ds(pl.multiple_of(branch * skel, skel), skel)
        matrix = matrices[level][:, cols]
        total = through(total, matrix)

    firsts = []
    made = 0
    for degree in range(levels + 1):
        firsts.append(made)
        made += max(1, share >> degree)
    totals = [total + far[firsts[levels]]]
    for degree in range(levels, 0, -1):
        first_row = leaf_count - 2 * (leaf_count >> degree)
        start = (member * share) >> degree
        child_start = (member * share) >> (degree - 1)
        children = max(1, share >> (degree - 1))
        after = []
        if children == 1:
            branch = child_start & 1
            cols = pl.ds(pl.multiple_of(branch * skel, skel), skel)
            after.append(through(totals[0], inner_maps[first_row + start, :, cols]) + far[firsts[degree - 1]])
        else:
            for c in range(children // 2):
                both = through(totals[c], inner_maps[first_row + start + c])
                after.append(both[:, :skel] + far[firsts[degree - 1] + 2 * c])
                after.append(both[:, skel:] + far[firsts[degree - 1] + 2 * c + 1])
        totals = after
    for c in range(share):
        out[:, c * leaf_size : (c + 1) * leaf_size] = (
            through(totals[c], leaf_maps[member * share + c]) + near[c]
        )


def on_device(
    points,
    charges,
    leaf_ids,
    inner_ids,
    upper_ids_first,
    upper_ids_second,
    upper_ids_third,
    leaf_maps,
    inner_maps,
    upper_maps_first,
    upper_maps_second,
    upper_maps_third,
    near_lists,
    far_inner,
    far_upper_first,
    far_upper_second,
    far_upper_third,
):
    dim, local_points = points.shape
    rhs = charges.shape[0]
    leaf_count, skel, leaf_size = leaf_maps.shape
    levels = leaf_count.bit_length() - 1
    stacked = dim + rhs
    depth = dim + NORM_ROWS
    subtrees = lax.axis_size("leaf")
    list_size = lax.axis_size("list")
    share = leaf_count // list_size
    scale = -3.0 / dim * math.log2(math.e)
    on_chip = [(i, i ^ 1) for i in range(subtrees)]
    across = [pair for i in range(1, subtrees - 1, 2) for pair in ((i, i + 1), (i + 1, i))]

    spot = jnp.stack([lax.axis_index("leaf"), lax.axis_index("list")]).astype(jnp.int32)
    mine = jnp.concatenate(
        [near_lists, far_inner, far_upper_first, far_upper_second, far_upper_third], axis=0
    )
    chunks = [mine] + [
        lax.ppermute(mine, "list", [(i, (i + shift) % list_size) for i in range(list_size)])
        for shift in range(1, list_size)
    ]
    uppers = (far_upper_first, far_upper_second, far_upper_third)
    plan = Plan(leaf_count, share, levels, list_size * mine.shape[1], [a.shape[0] for a in uppers])

    vmem = pl.BlockSpec(memory_space=pltpu.VMEM)
    smem = pl.BlockSpec(memory_space=pltpu.SMEM)
    anywhere = pl.BlockSpec(memory_space=pl.ANY)
    params = pltpu.CompilerParams(vmem_limit_bytes=VMEM_BYTES)

    def shaped(shape, dtype=BF):
        return jax.ShapeDtypeStruct(shape, dtype)

    def cost(flops, transcendentals=0):
        return pl.CostEstimate(flops=flops, bytes_accessed=4 * 10**6, transcendentals=transcendentals)

    inputs = (points, charges, leaf_ids, inner_ids, leaf_maps, inner_maps, upper_maps_first, upper_maps_second, upper_maps_third)
    block_rows = dim + sum(a.shape[0] for a in inputs[6:])
    bundle, extras, block = pl.pallas_call(
        functools.partial(up_body, levels),
        out_shape=(shaped((2 * leaf_count, stacked, leaf_size)), shaped((leaf_count // 2 + 1, stacked, leaf_size)), shaped((block_rows, 2 * skel))),
        in_specs=[anywhere] * 9,
        out_specs=(vmem, vmem, vmem),
        scratch_shapes=[pltpu.VMEM(a.shape, a.dtype) for a in inputs] + [pltpu.SemaphoreType.DMA((9,))],
        compiler_params=pltpu.CompilerParams(vmem_limit_bytes=UP_VMEM_BYTES),
        name="upward",
        cost_estimate=cost(10**11),
    )(*inputs)

    pair = lax.ppermute(bundle, "leaf", on_chip)
    def swapped(value, mask):
        return lax.ppermute(value, "leaf", [(i, i ^ mask) for i in range(subtrees)])

    sizes = [a.shape[0] for a in inputs[6:]]
    matrix_shape = shaped((skel, 2 * skel))

    def message_shape(level):
        rows = sum(dim << (level - k) for k in range(level + 1)) + sum(rows << (level + 1) for rows in sizes[level + 1 :])
        return shaped((rows, 2 * skel))

    table, first_message, first_matrix, slim = pl.pallas_call(
        functools.partial(table_body, plan, len(chunks), dim, sizes),
        out_shape=(shaped((plan.out_rows, LANES), jnp.int32), message_shape(0), matrix_shape, shaped((leaf_count + extras.shape[0], stacked, leaf_size))),
        in_specs=[smem] + [vmem] * len(chunks) + [anywhere] * 2 + [vmem] + [anywhere] * 2,
        out_specs=(vmem,) * 4,
        scratch_shapes=[pltpu.VMEM((LANES, LANES), jnp.int32), pltpu.VMEM((2, *block.shape), BF), pltpu.SemaphoreType.DMA((4,))],
        compiler_params=pltpu.CompilerParams(vmem_limit_bytes=UP_VMEM_BYTES),
        name="table",
        cost_estimate=cost(10**9),
    )(spot, *chunks, block, swapped(block, 1), upper_ids_first, bundle, extras)
    cross = lax.ppermute(slim, "leaf", across)

    acc_shapes = (shaped((share, rhs, leaf_size), F32), shaped((plan.targets, rhs, skel), F32))
    goal_shapes = (shaped((share, leaf_size, depth)), shaped((plan.targets, skel, depth)))

    def nodes_of(sides):
        return pltpu.VMEM((sides * plan.per_side, depth + rhs, skel), BF)

    far, far_goals = pl.pallas_call(
        functools.partial(far_body, plan, dim, scale),
        out_shape=(acc_shapes[1], goal_shapes[1]),
        in_specs=[smem, smem, anywhere, anywhere],
        out_specs=(vmem, vmem),
        scratch_shapes=[nodes_of(2), pltpu.SemaphoreType.DMA((2, 4))],
        compiler_params=params,
        name="far",
        cost_estimate=cost(10**10, 10**7),
    )(spot, table, bundle, pair)

    leaves_shape = shaped((2 * leaf_count, depth + rhs, leaf_size))
    near, near_goals, leaves, second_message, second_matrix = pl.pallas_call(
        functools.partial(near_body, plan, dim, sizes, scale),
        out_shape=(acc_shapes[0], goal_shapes[0], leaves_shape, message_shape(1), matrix_shape),
        in_specs=[smem, smem] + [anywhere] * 2 + [vmem] * 3 + [anywhere],
        out_specs=(vmem,) * 5,
        scratch_shapes=[pltpu.SemaphoreType.DMA((2, 2))],
        compiler_params=params,
        name="near",
        cost_estimate=cost(10**10),
    )(spot, table, bundle, pair, first_message, swapped(first_message, 2), upper_ids_second, far)

    near = pl.pallas_call(
        functools.partial(near_rest_body, plan, dim, scale),
        out_shape=acc_shapes[0],
        in_specs=[smem] + [vmem] * 3,
        out_specs=vmem,
        compiler_params=params,
        name="nearrest",
        cost_estimate=cost(10**7),
    )(table, near, near_goals, leaves)

    far, third_message, third_matrix = pl.pallas_call(
        functools.partial(cross_far_body, plan, dim, sizes, scale),
        out_shape=(acc_shapes[1], message_shape(2), matrix_shape),
        in_specs=[smem, smem, anywhere] + [vmem] * 5 + [anywhere],
        out_specs=(vmem,) * 3,
        scratch_shapes=[
            nodes_of(1),
            pltpu.VMEM((leaf_count, dim, leaf_size), BF),
            pltpu.VMEM((leaf_count, leaf_size), BF),
            pltpu.SemaphoreType.DMA((6,)),
        ],
        compiler_params=params,
        name="crossfar",
        cost_estimate=cost(10**10, 10**7),
    )(spot, table, cross, far, far_goals, second_message, swapped(second_message, 4), upper_ids_third, near)

    pieces = [third_message] + [swapped(third_message, mask) for mask in range(8, subtrees, 8)]

    near = pl.pallas_call(
        functools.partial(cross_near_body, plan, dim, scale),
        out_shape=acc_shapes[0],
        in_specs=[smem, anywhere, vmem, vmem, anywhere],
        out_specs=vmem,
        scratch_shapes=[pltpu.VMEM((leaf_count, depth + rhs, leaf_size), BF), pltpu.SemaphoreType.DMA((2,))],
        compiler_params=params,
        name="crossnear",
        cost_estimate=cost(10**10, 10**7),
    )(table, cross, near, near_goals, far)

    return pl.pallas_call(
        functools.partial(down_body, plan, dim, scale),
        out_shape=shaped((rhs, share * leaf_size), F32),
        in_specs=[smem, smem] + [vmem] * (len(pieces) + 7),
        out_specs=vmem,
        scratch_shapes=[
            pltpu.VMEM((sum(plan.upper_counts), depth + rhs, skel), BF),
            pltpu.VMEM((len(uppers), skel, depth), BF),
            pltpu.VMEM((len(uppers), rhs, skel), F32),
        ],
        compiler_params=params,
        name="down",
        cost_estimate=cost(10**9, 10**6),
    )(spot, table, *pieces, first_matrix, second_matrix, third_matrix, far, near, inner_maps, leaf_maps)


def solution(mesh):
    placed = (
        P(None, "leaf"),
        P(None, "leaf"),
        P("leaf", None),
        P("leaf", None),
        P(),
        P(),
        P(),
        P("leaf", None, None),
        P("leaf", None, None),
        P("leaf", None),
        P("leaf", None),
        P("leaf", None),
        P("leaf", "list"),
        P("leaf", "list"),
        P(None, "list"),
        P(None, "list"),
        P(None, "list"),
    )
    return jax.shard_map(
        on_device, mesh=mesh, in_specs=placed, out_specs=P(None, ("leaf", "list")), check_vma=False
    )
```
